32 devices in a mesh: kz: 4 (over z), en: 8 (over y, x, core).
Axes of the slice: x: 2, y: 2, z: 4, core: 2. Of those that a mesh axis runs over, the one named last changes fastest.
Arguments:
- green_lesser: bfloat16 [4, 16, 2, 512, 512], P('kz', 'en'), may hold values from -6 to 6
- coupling: float32 [3, 4, 2, 128, 128], replicated, may hold values from -0.25 to 0.25
- block_list: int32 [3, 4, 2], replicated, may hold values from 0 to 3, as said below
- offsets: int32 [3], replicated, may hold values from -1 to 1, as said below
- shifts: int32 [3], replicated, may hold values from 1 to 2, as said below
- occupation: float32 [3], replicated, may hold values from 0.25 to 4
Outputs:
- sigma_lesser: float32 [4, 16, 2, 512, 512], P('kz', 'en')
The draws below stay inside these ranges and needn't reach their ends.
Inputs may be any that keep to these rules, and one draw needn't show every extreme that they name: `block_list`: for each transfer, the 4 listed blocks hold every block row once and every block column once. -1 and +1 each occur among the offsets. 1 and 2 each occur among the shifts.
All inputs are finite; a program needn't handle non-finite values.
Results may differ from the reference program's by a relative error of at most 0.0057.
Values may be sent and summed in bfloat16 or wider, within the bound.
No kernel may reach another device: no remote copies, remote signals or barrier semaphores. Data moves between devices by JAX's collectives and lax.ppermute only.
A program may use at most 128 MiB of HBM per device.

```python
import math
import jax
import jax.numpy as jnp
from jax import lax

O = 512
BS = 128
NB = 4
NQ = 3
SMAX = 2
NK = 4
NE = 16


def draw_block_list(key, part):
    transfer_keys = jax.random.split(jax.random.fold_in(key, 101), NQ)

    def draw_single(subkey):
        row_key, column_key = jax.random.split(subkey)
        row_order = jax.random.permutation(row_key, NB)
        column_order = jax.random.permutation(column_key, NB)
        return jnp.stack([row_order, column_order], axis=1).astype(jnp.int32)
    return jax.vmap(draw_single)(transfer_keys)


def draw_offsets(key, part):
    place_key = jax.random.fold_in(key, 202)
    value_key = jax.random.fold_in(key, 203)
    positions = jax.random.permutation(place_key, NQ)
    values = jax.random.randint(value_key, (NQ,), -1, 2)
    values = values.at[positions[0]].set(-1)
    values = values.at[positions[1]].set(1)
    return values.astype(jnp.int32)


def draw_shifts(key, part):
    place_key = jax.random.fold_in(key, 302)
    value_key = jax.random.fold_in(key, 303)
    positions = jax.random.permutation(place_key, NQ)
    values = jax.random.randint(value_key, (NQ,), 1, SMAX + 1)
    values = values.at[positions[0]].set(SMAX)
    values = values.at[positions[1]].set(1)
    return values.astype(jnp.int32)


def block_levels(own_key, extent, pieces, smallest, high):
    gain = 1.0
    for axis_at, shards_of in pieces:
        heights = jax.random.uniform(jax.random.fold_in(jax.random.fold_in(own_key, 6), axis_at), (shards_of,), jnp.float32, smallest / len(pieces), high / len(pieces))
        gain = gain * jnp.repeat(jnp.exp(heights), extent[axis_at] // shards_of).reshape((-1,) + (1,) * (len(extent) - 1 - axis_at))
    return gain


def normal_values(key, dims, width, reach, cuts=(), kind=jnp.bfloat16):
    factor_of = block_levels(key, dims, cuts, -0.22, 0.18) if cuts else 1.0
    array = jax.random.normal(key, dims, jnp.float32) * width * factor_of
    return jnp.minimum(jnp.maximum(array, -reach), reach).astype(kind)


def setup_inputs(seed: int = 0) -> dict:
    key_list = jax.random.split(jax.random.key(seed), 7)
    green_lesser = normal_values(key_list[0], (NK, NE, 2, O, O), 1.0, 6.0, ((0, 4), (1, 8)))
    coupling = normal_values(key_list[1], (NQ, NB, 2, BS, BS), O ** -0.5, 0.25, (), jnp.float32)
    block_list = draw_block_list(jax.random.fold_in(key_list[6], 71), 0)
    offsets = draw_offsets(jax.random.fold_in(key_list[6], 71), 0)
    shifts = draw_shifts(jax.random.fold_in(key_list[6], 71), 0)
    occupation = jnp.clip(jnp.exp(jax.random.uniform(key_list[5], (NQ,), jnp.float32, math.log(0.25), math.log(4.0))), 0.25, 4.0)
    return dict(green_lesser=green_lesser, coupling=coupling, block_list=block_list, offsets=offsets, shifts=shifts, occupation=occupation)


def sandwich(field, blocks, row_index, column_index):
    batch_count = field.shape[0]
    orbitals = field.shape[-1]
    block_size = blocks.shape[-1]
    block_count = orbitals // block_size
    highest = lax.Precision.HIGHEST
    real_part = blocks[:, 0].astype(jnp.float32)
    imag_part = blocks[:, 1].astype(jnp.float32)
    placement = (row_index[:, None] == jnp.arange(block_count, dtype=jnp.int32)[None, :]).astype(jnp.float32)
    row_blocks = field.reshape(batch_count, 2, block_count, block_size, orbitals)
    picked = jnp.take(row_blocks, column_index, axis=2).astype(jnp.float32)

    def product_left(matrix, other):
        return jnp.einsum('nxy,lnyo->lnxo', matrix, other, precision=highest)

    left_real = product_left(real_part, picked[:, 0]) - product_left(imag_part, picked[:, 1])
    left_imag = product_left(real_part, picked[:, 1]) + product_left(imag_part, picked[:, 0])
    products = jnp.stack([left_real, left_imag], axis=1)
    left_half = jnp.einsum('na,lcnxo->lcaxo', placement, products, precision=highest)
    left_half = left_half.reshape(batch_count, 2, orbitals, orbitals).astype(jnp.bfloat16)
    column_blocks = left_half.reshape(batch_count, 2, orbitals, block_count, block_size)
    chosen = jnp.take(column_blocks, column_index, axis=3).astype(jnp.float32)

    def product_right(other, matrix):
        return jnp.einsum('lony,nxy->lonx', other, matrix, precision=highest)

    right_real = product_right(chosen[:, 0], real_part) + product_right(chosen[:, 1], imag_part)
    right_imag = product_right(chosen[:, 1], real_part) - product_right(chosen[:, 0], imag_part)
    stacked = jnp.stack([right_real, right_imag], axis=1)
    result = jnp.einsum('na,lconx->lcoax', placement, stacked, precision=highest)
    return result.reshape(batch_count, 2, orbitals, orbitals)


def reference(green_lesser, coupling, block_list, offsets, shifts, occupation):
    coupling_rounded = coupling.astype(jnp.bfloat16)
    momenta = green_lesser.shape[0]
    energies = green_lesser.shape[1]
    padded = jnp.pad(green_lesser, ((0, 0), (SMAX, SMAX), (0, 0), (0, 0), (0, 0)))

    def one_momentum(momentum):
        sigma_sum = jnp.zeros(green_lesser.shape[1:], jnp.float32)
        for transfer in range(NQ):
            source = jnp.mod(momentum - offsets[transfer], momenta).astype(jnp.int32)
            source_row = lax.dynamic_index_in_dim(padded, source, 0, keepdims=False)
            absorbed = lax.dynamic_slice_in_dim(source_row, (SMAX - shifts[transfer]).astype(jnp.int32), energies, 0)
            emitted = lax.dynamic_slice_in_dim(source_row, (SMAX + shifts[transfer]).astype(jnp.int32), energies, 0)
            weight = occupation[transfer]
            combined = (weight * absorbed.astype(jnp.float32) + (weight + 1.0) * emitted.astype(jnp.float32)).astype(jnp.bfloat16)
            sigma_sum = sigma_sum + sandwich(combined, coupling_rounded[transfer], block_list[transfer, :, 0], block_list[transfer, :, 1])
        return sigma_sum

    return lax.map(one_momentum, jnp.arange(momenta, dtype=jnp.int32))
```

```python
import functools

import jax
import jax.numpy as jnp
from jax import lax
from jax.experimental import pallas as pl
from jax.experimental.pallas import tpu as pltpu
from jax.sharding import PartitionSpec as P

SMAX = 2
VMEM_LIMIT = 56 * 1024 * 1024


def ring(count, step, periodic):
    pairs = [(i, i + step) for i in range(count) if 0 <= i + step < count]
    if periodic:
        pairs += [(i, (i + step) % count) for i in range(count) if not 0 <= i + step < count]
    return pairs


def whole(count):
    return [pl.BlockSpec(memory_space=pltpu.VMEM)] * count


def scalars(count):
    return [pl.BlockSpec(memory_space=pltpu.SMEM)] * count


def factors_kernel(coupling_ref, left_ref, right_ref):
    block = coupling_ref.shape[-1]
    real = coupling_ref[0, 0, 0]
    imag = coupling_ref[0, 0, 1]
    real_t = real.T
    imag_t = imag.T
    low, high = pl.ds(0, block), pl.ds(block, block)

    def put(ref, rows, columns, value):
        ref[0, 0, rows, columns] = value.astype(jnp.bfloat16)

    put(left_ref, low, low, real)
    put(left_ref, low, high, -imag)
    put(left_ref, high, low, imag)
    put(left_ref, high, high, real)
    put(right_ref, low, low, real_t)
    put(right_ref, low, high, -imag_t)
    put(right_ref, high, low, imag_t)
    put(right_ref, high, high, real_t)


def factors(coupling):
    transfers, listed, _, block, _ = coupling.shape
    shape = jax.ShapeDtypeStruct((transfers, listed, 2 * block, 2 * block), jnp.bfloat16)
    out_spec = pl.BlockSpec((1, 1, 2 * block, 2 * block), lambda q, n: (q, n, 0, 0))
    return pl.pallas_call(
        factors_kernel,
        grid=(transfers, listed),
        in_specs=[pl.BlockSpec((1, 1, 2, block, block), lambda q, n: (q, n, 0, 0, 0))],
        out_specs=[out_spec, out_spec],
        out_shape=[shape, shape],
        name="factors",
    )(coupling)


def sandwich(left_ref, right_ref, q, lists_ref, mixed, half, total):
    listed, rows = left_ref.shape[1], left_ref.shape[2] // 2

    def entry(n, side):
        return lists_ref[(q * listed + n) * 2 + side]

    for n in range(listed):
        product = jnp.dot(left_ref[q, n], mixed[entry(n, 1)], preferred_element_type=jnp.float32)
        product = product.astype(jnp.bfloat16)
        target = pl.ds(pl.multiple_of(entry(n, 0) * rows, rows), rows)
        for column in range(listed):
            for part in range(2):
                half[column, target, pl.ds(part * rows, rows)] = product[
                    part * rows : (part + 1) * rows, column * rows : (column + 1) * rows
                ]
    for n in range(listed):
        total[entry(n, 0)] += jnp.dot(half[entry(n, 1)], right_ref[q, n], preferred_element_type=jnp.float32)


def accumulate(energy, groups, scalar_refs, left_ref, right_ref, mixed, half, total):
    lists_ref, offsets_ref, shifts_ref, occupation_ref = scalar_refs
    total[...] = jnp.zeros_like(total)

    @pl.loop(0, left_ref.shape[0])
    def _(q):
        weight = occupation_ref[q]
        listed, rows = left_ref.shape[1], left_ref.shape[2] // 2
        for offset, levels in groups:
            for shift in range(1, SMAX + 1):
                first, second = levels[energy - shift + SMAX], levels[energy + shift + SMAX]

                @pl.when((offsets_ref[q] == offset) & (shifts_ref[q] == shift))
                def _():
                    for m in range(listed):
                        for part in range(2):
                            here = pl.ds(m * rows, rows)
                            a = first[0][0, first[1], part, here, :].astype(jnp.float32)
                            b = second[0][0, second[1], part, here, :].astype(jnp.float32)
                            mixed[m, pl.ds(part * rows, rows), :] = (weight * a + (weight + 1.0) * b).astype(
                                jnp.bfloat16
                            )

        wanted = functools.reduce(lambda x, y: x | y, [offsets_ref[q] == offset for offset, _ in groups])

        @pl.when(wanted)
        def _():
            sandwich(left_ref, right_ref, q, lists_ref, mixed, half, total)


def scratch(listed, block):
    return [
        pltpu.VMEM((listed, 2 * block, listed * block), jnp.bfloat16),
        pltpu.VMEM((listed, listed * block, 2 * block), jnp.bfloat16),
        pltpu.VMEM((listed, listed * block, 2 * block), jnp.float32),
    ]


def message_kernel(energy, offset, pick, *refs):
    scalar_refs, refs = refs[:4], refs[4:]
    left_ref, right_ref, *sources = refs[: -4]
    message_ref, mixed, half, total = refs[-4:]
    accumulate(energy, [(offset, pick(sources))], scalar_refs, left_ref, right_ref, mixed, half, total)
    message_ref[...] = total[...].astype(jnp.bfloat16)


def result_kernel(energies, picks, *refs):
    scalar_refs, refs = refs[:4], refs[4:]
    left_ref, right_ref, *sources = refs[: -5]
    arrived, out_ref, mixed, half, total = refs[-5:]
    block = left_ref.shape[2] // 2
    for energy in range(energies):
        groups = [(offset, pick(sources)) for offset, pick in picks]
        accumulate(energy, groups, scalar_refs, left_ref, right_ref, mixed, half, total)
        for column in range(left_ref.shape[1]):
            for part in range(2):
                value = total[column, :, pl.ds(part * block, block)]
                if energy == 0:
                    value = value + arrived[column, :, pl.ds(part * block, block)].astype(jnp.float32)
                out_ref[0, energy, part, :, pl.ds(column * block, block)] = value


def final_kernel(sum_ref, arrived_ref, out_ref):
    block = arrived_ref.shape[-1] // 2
    for part in range(2):
        out_ref[0, 0, part] = sum_ref[0, 0, part] + arrived_ref[0, :, pl.ds(part * block, block)].astype(jnp.float32)


def final(energy, sums, arrived):
    listed, orbitals, _ = arrived.shape
    block = orbitals // listed
    sum_spec = pl.BlockSpec((1, 1, 2, orbitals, block), lambda c: (0, energy, 0, 0, c))
    return pl.pallas_call(
        final_kernel,
        grid=(listed,),
        in_specs=[sum_spec, pl.BlockSpec((1, orbitals, 2 * block), lambda c: (c, 0, 0))],
        out_specs=sum_spec,
        out_shape=jax.ShapeDtypeStruct(sums.shape, sums.dtype),
        input_output_aliases={0: 0},
        name="final",
    )(sums, arrived)


def on_device(green_lesser, coupling, block_list, offsets, shifts, occupation):
    _, energies, _, orbitals, _ = green_lesser.shape
    listed, block = coupling.shape[1], coupling.shape[-1]
    assert green_lesser.shape[0] == 1 and energies == SMAX
    momenta, ranks = lax.axis_size("kz"), lax.axis_size("en")
    up, down = ring(ranks, 1, False), ring(ranks, -1, False)

    near = lax.ppermute(green_lesser, "kz", ring(momenta, -1, True))
    low = lax.ppermute(green_lesser, "en", up)
    high0 = lax.ppermute(green_lesser[:, :1], "en", down)
    high1 = lax.ppermute(green_lesser[:, 1:], "en", down)
    left, right = factors(coupling)
    scalar_args = (block_list.reshape(-1), offsets, shifts, occupation)

    def message(energy, sources, pick):
        return pl.pallas_call(
            functools.partial(message_kernel, energy, 1, pick),
            in_specs=scalars(4) + whole(2 + len(sources)),
            out_specs=pl.BlockSpec(memory_space=pltpu.VMEM),
            out_shape=jax.ShapeDtypeStruct((listed, orbitals, 2 * block), jnp.bfloat16),
            scratch_shapes=scratch(listed, block),
            compiler_params=pltpu.CompilerParams(vmem_limit_bytes=VMEM_LIMIT),
            cost_estimate=pl.CostEstimate(flops=10**9, bytes_accessed=10 * 2**20, transcendentals=0),
            name="message%d" % energy,
        )(*scalar_args, left, right, *sources)

    forward = ring(momenta, 1, True)

    def pick0(refs):
        own, low, high0 = refs
        return [(low, 0), (low, 1), (own, 0), (own, 1), (high0, 0), None]

    def pick1(refs):
        own, low, high0, high1 = refs
        return [(low, 0), (low, 1), (own, 0), (own, 1), (high0, 0), (high1, 0)]

    sent0 = message(0, (green_lesser, low, high0), pick0)
    arrived0 = lax.ppermute(sent0, "kz", forward)
    near_low = lax.ppermute(near, "en", up)
    near_high = lax.ppermute(near, "en", down)
    sent1 = message(1, (green_lesser, low, high0, high1), pick1)
    arrived1 = lax.ppermute(sent1, "kz", forward)

    def pick_own(refs):
        return pick1(refs[:4])

    def pick_near(refs):
        own, low, high = refs[4:]
        return [(low, 0), (low, 1), (own, 0), (own, 1), (high, 0), (high, 1)]

    sums = pl.pallas_call(
        functools.partial(result_kernel, energies, [(0, pick_own), (-1, pick_near)]),
        in_specs=scalars(4) + whole(10),
        out_specs=pl.BlockSpec(memory_space=pltpu.VMEM),
        out_shape=jax.ShapeDtypeStruct(green_lesser.shape, jnp.float32),
        scratch_shapes=scratch(listed, block),
        compiler_params=pltpu.CompilerParams(vmem_limit_bytes=VMEM_LIMIT),
        cost_estimate=pl.CostEstimate(flops=2 * 10**9, bytes_accessed=20 * 2**20, transcendentals=0),
        name="result",
    )(*scalar_args, left, right, green_lesser, low, high0, high1, near, near_low, near_high, arrived0)
    return final(1, sums, arrived1)


def solution(mesh):
    placed = (P("kz", "en", None, None, None), P(), P(), P(), P(), P())
    return jax.shard_map(
        on_device,
        mesh=mesh,
        in_specs=placed,
        out_specs=P("kz", "en", None, None, None),
        check_vma=False,
    )
```

```python
import functools

import jax
import jax.numpy as jnp
from jax import lax
from jax.experimental import pallas as pl
from jax.experimental.pallas import tpu as pltpu
from jax.sharding import PartitionSpec as P

SMAX = 2
VMEM_LIMIT = 16 * 1024 * 1024
ANY = pl.BlockSpec(memory_space=pl.ANY)
SMEM = pl.BlockSpec(memory_space=pltpu.SMEM)
VMEM = pl.BlockSpec(memory_space=pltpu.VMEM)
PARAMS = pltpu.CompilerParams(vmem_limit_bytes=VMEM_LIMIT)
CHEAP = pl.CostEstimate(flops=1, bytes_accessed=1, transcendentals=0)


def ring(count, step, periodic):
    pairs = [(i, i + step) for i in range(count) if 0 <= i + step < count]
    if periodic:
        pairs += [(i, (i + step) % count) for i in range(count) if not 0 <= i + step < count]
    return pairs


def pinned(x):
    return pltpu.with_memory_space_constraint(x, pltpu.VMEM)


def after(value, *earlier):
    return pl.pallas_call(
        lambda *refs: None,
        in_specs=[ANY] * (1 + len(earlier)),
        out_specs=ANY,
        out_shape=jax.ShapeDtypeStruct(value.shape, value.dtype),
        input_output_aliases={0: 0},
        compiler_params=PARAMS,
        cost_estimate=CHEAP,
        name="after",
    )(value, *earlier)


def take_kernel(energy, green_ref, out_ref, sem):
    copy = pltpu.make_async_copy(green_ref.at[:, pl.ds(energy, 1)], out_ref, sem)
    copy.start()
    copy.wait()


def take(green, energy):
    return pl.pallas_call(
        functools.partial(take_kernel, energy),
        in_specs=[ANY],
        out_specs=VMEM,
        out_shape=pltpu.VMEM((1, 1, *green.shape[2:]), green.dtype),
        scratch_shapes=[pltpu.SemaphoreType.DMA],
        compiler_params=PARAMS,
        cost_estimate=CHEAP,
        name="take",
    )(green)


def prepare_kernel(energy, green_ref, coupling_ref, out_ref, left_ref, right_ref, sem):
    copy = pltpu.make_async_copy(green_ref.at[:, pl.ds(energy, 1)], out_ref, sem)
    copy.start()
    transfers, listed, _, block, _ = coupling_ref.shape
    low, high = pl.ds(0, block), pl.ds(block, block)

    @pl.loop(0, transfers)
    def _(q):
        for n in range(listed):
            real, imag = coupling_ref[q, n, 0], coupling_ref[q, n, 1]
            for ref, a, b in ((left_ref, real, imag), (right_ref, real.T, imag.T)):
                ref[q, n, low, low] = a.astype(jnp.bfloat16)
                ref[q, n, low, high] = (-b).astype(jnp.bfloat16)
                ref[q, n, high, low] = b.astype(jnp.bfloat16)
                ref[q, n, high, high] = a.astype(jnp.bfloat16)

    copy.wait()


def prepare(green, energy, coupling):
    transfers, listed, _, block, _ = coupling.shape
    factor = pltpu.VMEM((transfers, listed, 2 * block, 2 * block), jnp.bfloat16)
    return pl.pallas_call(
        functools.partial(prepare_kernel, energy),
        in_specs=[ANY, VMEM],
        out_specs=[VMEM, VMEM, VMEM],
        out_shape=[pltpu.VMEM((1, 1, *green.shape[2:]), green.dtype), factor, factor],
        scratch_shapes=[pltpu.SemaphoreType.DMA],
        compiler_params=PARAMS,
        cost_estimate=CHEAP,
        name="prepare",
    )(green, coupling)


class Terms:
    def __init__(self, scalar_refs, factor_refs, scratch):
        self.lists, self.offsets, self.shifts, self.occupation = scalar_refs
        self.left, self.right = factor_refs
        self.mixed, self.half = scratch
        self.transfers, self.listed = self.left.shape[0], self.left.shape[1]
        self.block = self.left.shape[2] // 2

    def entry(self, q, n, side):
        return self.lists[(q * self.listed + n) * 2 + side]

    def mix(self, q, first, second):
        weight = self.occupation[q]
        block = self.block

        @pl.loop(0, self.listed)
        def _(m):
            here = pl.ds(pl.multiple_of(m * block, block), block)
            for part in range(2):
                a = first[part, here, :].astype(jnp.float32)
                b = second[part, here, :].astype(jnp.float32)
                self.mixed[m, pl.ds(part * block, block), :] = (weight * a + (weight + 1.0) * b).astype(jnp.bfloat16)

    def multiply(self, q, emit):
        block = self.block
        for n in range(self.listed):
            product = jnp.dot(self.left[q, n], self.mixed[self.entry(q, n, 1)], preferred_element_type=jnp.float32)
            product = product.astype(jnp.bfloat16)
            target = pl.ds(pl.multiple_of(self.entry(q, n, 0) * block, block), block)
            for column in range(self.listed):
                for part in range(2):
                    self.half[column, target, pl.ds(part * block, block)] = product[
                        part * block : (part + 1) * block, column * block : (column + 1) * block
                    ]
        for n in range(self.listed):
            product = jnp.dot(self.half[self.entry(q, n, 1)], self.right[q, n], preferred_element_type=jnp.float32)
            emit(self.entry(q, n, 0), product)


def term_scratch(coupling_shape, orbitals):
    _, listed, _, block, _ = coupling_shape
    return [
        pltpu.VMEM((listed, 2 * block, orbitals), jnp.bfloat16),
        pltpu.VMEM((listed, orbitals, 2 * block), jnp.bfloat16),
    ]


def pair_of(energy, shift, own0, own1, low, high0, high1):
    last = None if high1 is None else high1.at[0, 0]
    levels = [low.at[0, 0], low.at[0, 1], own0.at[0, 0], own1.at[0, 0], high0.at[0, 0], last]
    return levels[energy - shift + SMAX], levels[energy + shift + SMAX]


def message_kernel(energy, offset, *refs):
    terms = Terms(refs[:4], refs[4:6], refs[-2:])
    own0, own1, low, high0 = refs[6:10]
    high1 = refs[10] if energy else None
    message_ref, total = refs[-4:-2]
    total[...] = jnp.zeros_like(total)

    @pl.loop(0, terms.transfers)
    def _(q):
        wanted = terms.offsets[q] == offset
        for shift in range(1, SMAX + 1):

            @pl.when(wanted & (terms.shifts[q] == shift))
            def _():
                terms.mix(q, *pair_of(energy, shift, own0, own1, low, high0, high1))

        @pl.when(wanted)
        def _():
            def emit(place, product):
                total[place] += product

            terms.multiply(q, emit)

    message_ref[...] = total[...].astype(jnp.bfloat16)


def add_to(total, energy, block):
    def emit(place, product):
        columns = pl.ds(pl.multiple_of(place * block, block), block)
        for part in range(2):
            total[0, energy, part, :, columns] += product[:, part * block : (part + 1) * block]

    return emit


def first_kernel(own_offset, near_offset, *refs):
    terms = Terms(refs[:4], refs[4:6], refs[-2:])
    own0, own1, low, high0, high1, near0, near_low0, near_high0, total = refs[6:-2]
    energies = total.shape[1]
    total[...] = jnp.zeros_like(total)
    near_sources = {1: near0, 2: near_low0}

    @pl.loop(0, terms.transfers * energies)
    def _(step):
        q = step // energies
        energy = step - q * energies
        own = terms.offsets[q] == own_offset
        near = (terms.offsets[q] == near_offset) & (energy == SMAX - terms.shifts[q])
        for shift in range(1, SMAX + 1):

            @pl.when(near & (terms.shifts[q] == shift))
            def _():
                terms.mix(q, near_sources[shift].at[0, 0], near_high0.at[0, 0])

            for e in range(energies):

                @pl.when(own & (terms.shifts[q] == shift) & (energy == e))
                def _():
                    terms.mix(q, *pair_of(e, shift, own0, own1, low, high0, high1))

        @pl.when(own | near)
        def _():
            terms.multiply(q, add_to(total, energy, terms.block))


def second_kernel(near_offset, *refs):
    terms = Terms(refs[:4], refs[4:6], refs[-3:-1])
    sum_ref, arrived, near1, near_low1, near_high1, total, out_ref = refs[6:-3]
    sem = refs[-1]
    block = terms.block
    total[0, 1] = sum_ref[0, 1]
    for column in range(terms.listed):
        columns = pl.ds(column * block, block)
        for part in range(2):
            total[0, 0, part, :, columns] = sum_ref[0, 0, part, :, columns] + arrived[
                column, :, pl.ds(part * block, block)
            ].astype(jnp.float32)
    near_sources = {1: near1, 2: near_high1}

    @pl.loop(0, terms.transfers)
    def _(q):
        near = terms.offsets[q] == near_offset
        for shift in range(1, SMAX + 1):

            @pl.when(near & (terms.shifts[q] == shift))
            def _():
                terms.mix(q, near_low1.at[0, 0], near_sources[shift].at[0, 0])

        @pl.when(near)
        def _():
            terms.multiply(q, add_to(total, terms.shifts[q] - 1, block))

    copy = pltpu.make_async_copy(total.at[:, pl.ds(0, 1)], out_ref.at[:, pl.ds(0, 1)], sem)
    copy.start()
    copy.wait()


def final_kernel(sum_ref, arrived, _, out_ref, held, sems):
    listed, orbitals, width = arrived.shape
    block = width // 2
    copies = []
    for piece in range(orbitals // block):
        rows = pl.ds(piece * block, block)
        for column in range(listed):
            columns = pl.ds(column * block, block)
            for part in range(2):
                held[part, rows, columns] = sum_ref[0, 1, part, rows, columns] + arrived[
                    column, rows, pl.ds(part * block, block)
                ].astype(jnp.float32)
        copies.append(pltpu.make_async_copy(held.at[:, rows, :], out_ref.at[0, 1, :, rows, :], sems.at[piece]))
        copies[-1].start()
    for copy in copies:
        copy.wait()


def on_device(green_lesser, coupling, block_list, offsets, shifts, occupation):
    _, energies, _, orbitals, _ = green_lesser.shape
    transfers, listed, _, block, _ = coupling.shape
    assert green_lesser.shape[0] == 1 and energies == SMAX
    momenta, ranks = lax.axis_size("kz"), lax.axis_size("en")
    up, down = ring(ranks, 1, False), ring(ranks, -1, False)
    forward, backward = ring(momenta, 1, True), ring(momenta, -1, True)
    scalar_args = (block_list.reshape(-1), offsets, shifts, occupation)
    result = jax.ShapeDtypeStruct(green_lesser.shape, jnp.float32)
    result_held = pltpu.VMEM(green_lesser.shape, jnp.float32)

    green0 = take(green_lesser, 0)
    near0 = lax.ppermute(green0, "kz", backward)
    low = lax.ppermute(green_lesser, "en", up)
    high0 = lax.ppermute(green0, "en", down)
    green1, left, right = prepare(green_lesser, 1, coupling)
    near1 = lax.ppermute(green1, "kz", backward)
    high1 = lax.ppermute(green1, "en", down)
    near_low0 = lax.ppermute(near0, "en", up)
    near_high0 = lax.ppermute(near0, "en", down)
    factors = (pinned(left), pinned(right))

    def call(kernel, out_shape, scratch, name, *operands):
        out_specs = VMEM
        if isinstance(out_shape, tuple):
            out_specs = (VMEM, ANY)
        return pl.pallas_call(
            kernel,
            in_specs=[SMEM] * 4 + [VMEM] * (2 + len(operands)),
            out_specs=out_specs,
            out_shape=out_shape,
            scratch_shapes=scratch,
            compiler_params=PARAMS,
            cost_estimate=CHEAP,
            name=name,
        )(*scalar_args, *factors, *[pinned(x) for x in operands])

    def message(energy, *operands):
        total = pltpu.VMEM((listed, orbitals, 2 * block), jnp.float32)
        sent = pltpu.VMEM(total.shape, jnp.bfloat16)
        scratch = [total, *term_scratch(coupling.shape, orbitals)]
        return call(functools.partial(message_kernel, energy, 1), sent, scratch, "message%d" % energy, *operands)

    sent0 = message(0, green0, green1, low, high0)
    arrived0 = lax.ppermute(sent0, "kz", forward)
    near1 = after(near1, sent0)
    near_low1 = lax.ppermute(near1, "en", up)
    near_high1 = lax.ppermute(near1, "en", down)
    sent1 = message(1, green0, green1, low, high0, high1)
    arrived1 = lax.ppermute(sent1, "kz", forward)

    scratch = term_scratch(coupling.shape, orbitals)
    sums = call(
        functools.partial(first_kernel, 0, -1),
        result_held,
        scratch,
        "first",
        *(green0, green1, low, high0, high1, near0, near_low0, near_high0),
    )
    sums, partial = call(
        functools.partial(second_kernel, -1),
        (result_held, result),
        [*scratch, pltpu.SemaphoreType.DMA],
        "second",
        *(sums, arrived0, near1, near_low1, near_high1),
    )
    return pl.pallas_call(
        final_kernel,
        in_specs=[VMEM, VMEM, ANY],
        out_specs=ANY,
        out_shape=result,
        scratch_shapes=[
            pltpu.VMEM(green_lesser.shape[2:], jnp.float32),
            pltpu.SemaphoreType.DMA((orbitals // block,)),
        ],
        input_output_aliases={2: 0},
        compiler_params=PARAMS,
        cost_estimate=CHEAP,
        name="final",
    )(pinned(sums), pinned(arrived1), partial)


def solution(mesh):
    placed = (P("kz", "en", None, None, None), P(), P(), P(), P(), P())
    return jax.shard_map(
        on_device,
        mesh=mesh,
        in_specs=placed,
        out_specs=P("kz", "en", None, None, None),
        check_vma=False,
    )
```

```python
import functools

import jax
import jax.numpy as jnp
from jax import lax
from jax.experimental import pallas as pl
from jax.experimental.pallas import tpu as pltpu
from jax.sharding import PartitionSpec as P

SMAX = 2
PIECES = 4
VMEM_LIMIT = 12 * 1024 * 1024
ANY = pl.BlockSpec(memory_space=pl.ANY)
SMEM = pl.BlockSpec(memory_space=pltpu.SMEM)
VMEM = pl.BlockSpec(memory_space=pltpu.VMEM)
PARAMS = pltpu.CompilerParams(vmem_limit_bytes=VMEM_LIMIT)
DEAR = pl.CostEstimate(flops=2 * 10**11, bytes_accessed=1, transcendentals=0)
CHEAP = pl.CostEstimate(flops=1, bytes_accessed=1, transcendentals=0)


def ring(count, step):
    return [(i, (i + step) % count) for i in range(count)]


def both_ways(pairs):
    return [*pairs, *[(j, i) for i, j in pairs]]


def pinned(x):
    return pltpu.with_memory_space_constraint(x, pltpu.VMEM)


def after(value, *earlier):
    return pl.pallas_call(
        lambda *refs: None,
        in_specs=[ANY] * (1 + len(earlier)),
        out_specs=ANY,
        out_shape=jax.ShapeDtypeStruct(value.shape, value.dtype),
        input_output_aliases={0: 0},
        compiler_params=PARAMS,
        cost_estimate=DEAR,
        name="after",
    )(value, *earlier)


def odd():
    return lax.axis_index("en") % 2


def fetch(green_ref, energy, out_ref, sems):
    rows = out_ref.shape[1] // sems.shape[1]
    copies = []
    for part in range(sems.shape[0]):
        for piece in range(sems.shape[1]):
            here = pl.ds(piece * rows, rows)
            copies.append(
                pltpu.make_async_copy(
                    green_ref.at[0, energy, part, here, :], out_ref.at[part, here, :], sems.at[part, piece]
                )
            )
            copies[-1].start()
    return copies


def take_kernel(green_ref, out_ref, sems):
    for copy in fetch(green_ref, odd(), out_ref, sems):
        copy.wait()


def take(green):
    return pl.pallas_call(
        take_kernel,
        in_specs=[ANY],
        out_specs=VMEM,
        out_shape=pltpu.VMEM(green.shape[2:], green.dtype),
        scratch_shapes=[pltpu.SemaphoreType.DMA((2, PIECES))],
        compiler_params=PARAMS,
        cost_estimate=CHEAP,
        name="take",
    )(pltpu.with_memory_space_constraint(green, pltpu.HBM))


def prepare_kernel(green_ref, coupling_ref, _, out_ref, left_ref, right_ref, sems):
    copies = fetch(green_ref, 1 - odd(), out_ref, sems)
    transfers, listed, _, block, _ = coupling_ref.shape
    low, high = pl.ds(0, block), pl.ds(block, block)

    @pl.loop(0, transfers)
    def _(q):
        for n in range(listed):
            real, imag = coupling_ref[q, n, 0], coupling_ref[q, n, 1]
            for ref, a, b in ((left_ref, real, imag), (right_ref, real.T, imag.T)):
                ref[q, n, low, low] = a.astype(jnp.bfloat16)
                ref[q, n, low, high] = (-b).astype(jnp.bfloat16)
                ref[q, n, high, low] = b.astype(jnp.bfloat16)
                ref[q, n, high, high] = a.astype(jnp.bfloat16)

    for copy in copies:
        copy.wait()


def prepare(green, coupling, earlier):
    transfers, listed, _, block, _ = coupling.shape
    factor = pltpu.VMEM((transfers, listed, 2 * block, 2 * block), jnp.bfloat16)
    return pl.pallas_call(
        prepare_kernel,
        in_specs=[ANY, VMEM, ANY],
        out_specs=[VMEM, VMEM, VMEM],
        out_shape=[pltpu.VMEM(green.shape[2:], green.dtype), factor, factor],
        scratch_shapes=[pltpu.SemaphoreType.DMA((2, PIECES))],
        compiler_params=PARAMS,
        cost_estimate=CHEAP,
        name="prepare",
    )(pltpu.with_memory_space_constraint(green, pltpu.HBM), coupling, earlier)


class Terms:
    def __init__(self, scalar_refs, factor_refs, scratch):
        self.lists, self.offsets, self.shifts, self.occupation = scalar_refs
        self.left, self.right = factor_refs
        self.mixed, self.half = scratch
        self.transfers, self.listed = self.left.shape[0], self.left.shape[1]
        self.block = self.left.shape[2] // 2

    def entry(self, q, n, side):
        return self.lists[(q * self.listed + n) * 2 + side]

    def mix(self, q, first, second):
        away = self.occupation[q] + jnp.where(odd() == 1, 0.0, 1.0)
        towards = self.occupation[q] + jnp.where(odd() == 1, 1.0, 0.0)
        block = self.block

        @pl.loop(0, self.listed)
        def _(m):
            here = pl.ds(pl.multiple_of(m * block, block), block)
            for part in range(2):
                a = first[part, here, :].astype(jnp.float32)
                b = second[part, here, :].astype(jnp.float32)
                self.mixed[m, pl.ds(part * block, block), :] = (away * a + towards * b).astype(jnp.bfloat16)

    def multiply(self, q, emit):
        block = self.block
        for n in range(self.listed):
            product = jnp.dot(self.left[q, n], self.mixed[self.entry(q, n, 1)], preferred_element_type=jnp.float32)
            product = product.astype(jnp.bfloat16)
            target = pl.ds(pl.multiple_of(self.entry(q, n, 0) * block, block), block)
            for column in range(self.listed):
                for part in range(2):
                    self.half[column, target, pl.ds(part * block, block)] = product[
                        part * block : (part + 1) * block, column * block : (column + 1) * block
                    ]
        for n in range(self.listed):
            product = jnp.dot(self.half[self.entry(q, n, 1)], self.right[q, n], preferred_element_type=jnp.float32)
            emit(self.entry(q, n, 0), product)


def term_scratch(coupling_shape, orbitals):
    _, listed, _, block, _ = coupling_shape
    return [
        pltpu.VMEM((listed, 2 * block, orbitals), jnp.bfloat16),
        pltpu.VMEM((listed, orbitals, 2 * block), jnp.bfloat16),
    ]


def levels_of(chip_mate, *others):
    return (chip_mate.at[0, 1 - odd()], chip_mate.at[0, odd()], *others)


def pair_of(place, shift, levels):
    return levels[place - shift + SMAX], levels[place + shift + SMAX]


def message_kernel(place, offset, *refs):
    terms = Terms(refs[:4], refs[4:6], refs[-2:])
    levels = levels_of(*refs[6:-4])
    message_ref, total = refs[-4:-2]
    total[...] = jnp.zeros_like(total)

    @pl.loop(0, terms.transfers)
    def _(q):
        wanted = terms.offsets[q] == offset
        for shift in range(1, SMAX + 1):

            @pl.when(wanted & (terms.shifts[q] == shift))
            def _():
                terms.mix(q, *pair_of(place, shift, levels))

        @pl.when(wanted)
        def _():
            def emit(row, product):
                total[row] += product

            terms.multiply(q, emit)

    message_ref[...] = total[...].astype(jnp.bfloat16)


def add_to(total, block):
    def emit(row, product):
        columns = pl.ds(pl.multiple_of(row * block, block), block)
        for part in range(2):
            total[part, :, columns] += product[:, part * block : (part + 1) * block]

    return emit


def first_kernel(own_offset, near_offset, *refs):
    terms = Terms(refs[:4], refs[4:6], refs[-2:])
    own, near, totals = levels_of(*refs[6:11]), (*refs[11:16], None), refs[17:-2]
    for total in totals:
        total[...] = jnp.zeros_like(total)

    @pl.loop(0, terms.transfers)
    def _(q):
        is_own = terms.offsets[q] == own_offset
        is_near = terms.offsets[q] == near_offset
        for place, total in enumerate(totals):
            for shift in range(1, SMAX + 1):
                here = terms.shifts[q] == shift

                @pl.when(is_own & here)
                def _():
                    terms.mix(q, *pair_of(place, shift, own))

                if place + shift <= SMAX:

                    @pl.when(is_near & here)
                    def _():
                        terms.mix(q, *pair_of(place, shift, near))

            @pl.when(is_own | (is_near & (terms.shifts[q] + place <= SMAX)))
            def _():
                terms.multiply(q, add_to(total, terms.block))


def second_kernel(near_offset, *refs):
    terms = Terms(refs[:4], refs[4:6], refs[-2:])
    sum_ref, first, second, total = refs[6:-2]
    total[...] = sum_ref[...]

    @pl.loop(0, terms.transfers)
    def _(q):
        @pl.when((terms.offsets[q] == near_offset) & (terms.shifts[q] == SMAX))
        def _():
            terms.mix(q, first, second)
            terms.multiply(q, add_to(total, terms.block))


def store_kernel(place, sum_ref, arrived, *refs):
    out_ref, held, sems = refs[-3:]
    listed, orbitals, width = arrived.shape
    block = width // 2
    energy = odd() * place + (1 - odd()) * (1 - place)
    copies = []
    for piece in range(orbitals // block):
        rows = pl.ds(piece * block, block)
        for column in range(listed):
            columns = pl.ds(column * block, block)
            for part in range(2):
                held[part, rows, columns] = sum_ref[part, rows, columns] + arrived[
                    column, rows, pl.ds(part * block, block)
                ].astype(jnp.float32)
        copies.append(pltpu.make_async_copy(held.at[:, rows, :], out_ref.at[0, energy, :, rows, :], sems.at[piece]))
        copies[-1].start()
    for copy in copies:
        copy.wait()


def store(place, sums, arrived, result, *earlier):
    return pl.pallas_call(
        functools.partial(store_kernel, place),
        in_specs=[VMEM, VMEM] + [ANY] * len(earlier),
        out_specs=ANY,
        out_shape=result,
        scratch_shapes=[
            pltpu.VMEM(result.shape[2:], jnp.float32),
            pltpu.SemaphoreType.DMA((2 * arrived.shape[1] // arrived.shape[2],)),
        ],
        input_output_aliases={2: 0} if earlier else {},
        compiler_params=PARAMS,
        cost_estimate=CHEAP,
        name="store%d" % place,
    )(pinned(sums), pinned(arrived), *earlier)


def on_device(green_lesser, coupling, block_list, offsets, shifts, occupation):
    _, energies, _, orbitals, _ = green_lesser.shape
    transfers, listed, _, block, _ = coupling.shape
    assert green_lesser.shape[0] == 1 and energies == SMAX
    momenta, ranks = lax.axis_size("kz"), lax.axis_size("en")
    forward, backward = ring(momenta, 1), ring(momenta, -1)
    scalar_args = (block_list.reshape(-1), offsets, shifts, occupation)
    result = jax.ShapeDtypeStruct(green_lesser.shape, jnp.float32)
    held = pltpu.VMEM(green_lesser.shape[2:], jnp.float32)

    on_chip = both_ways([(i, i + 1) for i in range(0, ranks - 1, 2)])
    between = both_ways([(i, i + 1) for i in range(1, ranks - 1, 2)])

    def call(kernel, out_shape, name, *operands, scratch=()):
        return pl.pallas_call(
            kernel,
            in_specs=[SMEM] * 4 + [VMEM] * (2 + len(operands)),
            out_specs=[VMEM] * len(out_shape),
            out_shape=out_shape,
            scratch_shapes=[*scratch, *term_scratch(coupling.shape, orbitals)],
            compiler_params=PARAMS,
            cost_estimate=CHEAP,
            name=name,
        )(*scalar_args, pinned(left), pinned(right), *[pinned(x) for x in operands])

    def message(place, *operands):
        total = pltpu.VMEM((listed, orbitals, 2 * block), jnp.float32)
        sent = pltpu.VMEM(total.shape, jnp.bfloat16)
        kernel = functools.partial(message_kernel, place, 1)
        return call(kernel, [sent], "message%d" % place, *operands, scratch=[total])[0]

    own1 = take(green_lesser)
    near1 = lax.ppermute(own1, "kz", backward)
    own2 = lax.ppermute(own1, "en", between)
    own0, left, right = prepare(green_lesser, coupling, own1)
    near0 = lax.ppermute(own0, "kz", backward)
    own3 = lax.ppermute(own0, "en", between)
    own_ = lax.ppermute(green_lesser, "en", on_chip)
    own = (own_, own0, own1, own2, own3)

    sent0 = message(0, *own[:-1])
    arrived0 = lax.ppermute(sent0, "kz", forward)
    near1 = after(near1, sent0)
    near2 = lax.ppermute(near1, "en", between)
    mate1 = lax.ppermute(near1, "en", on_chip)

    sent1 = message(1, *own)
    arrived1 = lax.ppermute(sent1, "kz", forward)
    near0 = after(near0, sent1, mate1)
    near3 = lax.ppermute(near0, "en", between)
    mate0 = lax.ppermute(near0, "en", on_chip)

    first = functools.partial(first_kernel, 0, -1)
    sums0, sums1 = call(first, [held, held], "first", *own, mate1, mate0, near0, near1, near2, arrived0)
    partial = store(0, sums0, arrived0, result)
    second = functools.partial(second_kernel, -1)
    (sums1,) = call(second, [held], "second", sums1, mate0, near3)
    return store(1, sums1, arrived1, result, partial)


def solution(mesh):
    placed = (P("kz", "en", None, None, None), P(), P(), P(), P(), P())
    return jax.shard_map(
        on_device,
        mesh=mesh,
        in_specs=placed,
        out_specs=P("kz", "en", None, None, None),
        check_vma=False,
    )
```

```python
import functools
import math

import jax
import jax.numpy as jnp
from jax import lax
from jax.experimental import pallas as pl
from jax.experimental.pallas import tpu as pltpu
from jax.sharding import PartitionSpec as P

SMAX = 2
PIECES = 4
MIB = 1024 * 1024
SMALL = pltpu.CompilerParams(vmem_limit_bytes=6 * MIB)
LARGE = pltpu.CompilerParams(vmem_limit_bytes=24 * MIB)
ANY = pl.BlockSpec(memory_space=pl.ANY)
SMEM = pl.BlockSpec(memory_space=pltpu.SMEM)
VMEM = pl.BlockSpec(memory_space=pltpu.VMEM)
DEAR = pl.CostEstimate(flops=2 * 10**11, bytes_accessed=1, transcendentals=0)
CHEAP = pl.CostEstimate(flops=1, bytes_accessed=1, transcendentals=0)


def ring(count, step):
    return [(i, (i + step) % count) for i in range(count)]


def both_ways(pairs):
    return [*pairs, *[(j, i) for i, j in pairs]]


def in_vmem(x):
    return pltpu.with_memory_space_constraint(x, pltpu.VMEM)


def in_hbm(x):
    return pltpu.with_memory_space_constraint(x, pltpu.HBM)


def after(value, *earlier):
    return pl.pallas_call(
        lambda *refs: None,
        in_specs=[ANY] * (1 + len(earlier)),
        out_specs=ANY,
        out_shape=jax.ShapeDtypeStruct(value.shape, value.dtype),
        input_output_aliases={0: 0},
        compiler_params=SMALL,
        cost_estimate=DEAR,
        name="after",
    )(value, *earlier)


def odd():
    return lax.axis_index("en") % 2


def pieces_of(ref, count):
    rows = ref.shape[-2] // count
    return [(part, pl.ds(piece * rows, rows)) for part in range(2) for piece in range(count)]


def carry(green_ref, energy, out_ref, held, sems):
    places = pieces_of(held, PIECES)

    def copy(i, way):
        part, here = places[i]
        ends = (green_ref.at[0, energy, part, here, :], held.at[part, here, :], out_ref.at[part, here, :])
        return pltpu.make_async_copy(ends[way], ends[way + 1], sems.at[way, i])

    for i in range(len(places)):
        copy(i, 0).start()

    def finish():
        for i in range(len(places)):
            copy(i, 0).wait()
            copy(i, 1).start()
        for i in range(len(places)):
            copy(i, 1).wait()

    return finish


def carry_scratch(green):
    return [pltpu.VMEM(green.shape[2:], green.dtype), pltpu.SemaphoreType.DMA((2, 2 * PIECES))]


def take_kernel(green_ref, out_ref, sems):
    copies = []
    for i, (part, here) in enumerate(pieces_of(out_ref, PIECES)):
        copies.append(
            pltpu.make_async_copy(green_ref.at[0, odd(), part, here, :], out_ref.at[part, here, :], sems.at[i])
        )
        copies[-1].start()
    for copy in copies:
        copy.wait()


def take(green):
    return pl.pallas_call(
        take_kernel,
        in_specs=[ANY],
        out_specs=VMEM,
        out_shape=pltpu.VMEM(green.shape[2:], green.dtype),
        scratch_shapes=[pltpu.SemaphoreType.DMA((2 * PIECES,))],
        compiler_params=SMALL,
        cost_estimate=CHEAP,
        name="take",
    )(in_hbm(green))


def prepare_kernel(green_ref, coupling_ref, _, out_ref, left_ref, right_ref, held, sems):
    finish = carry(green_ref, 1 - odd(), out_ref, held, sems)
    transfers, listed, _, block, _ = coupling_ref.shape
    low, high = pl.ds(0, block), pl.ds(block, block)

    @pl.loop(0, transfers)
    def _(q):
        for n in range(listed):
            real, imag = coupling_ref[q, n, 0], coupling_ref[q, n, 1]
            for ref, a, b in ((left_ref, real, imag), (right_ref, real.T, imag.T)):
                ref[q, n, low, low] = a.astype(jnp.bfloat16)
                ref[q, n, low, high] = (-b).astype(jnp.bfloat16)
                ref[q, n, high, low] = b.astype(jnp.bfloat16)
                ref[q, n, high, high] = a.astype(jnp.bfloat16)

    finish()


def prepare(green, coupling, earlier):
    transfers, listed, _, block, _ = coupling.shape
    factor = pltpu.VMEM((transfers, listed, 2 * block, 2 * block), jnp.bfloat16)
    return pl.pallas_call(
        prepare_kernel,
        in_specs=[ANY, VMEM, ANY],
        out_specs=[ANY, VMEM, VMEM],
        out_shape=[jax.ShapeDtypeStruct(green.shape[2:], green.dtype), factor, factor],
        scratch_shapes=carry_scratch(green),
        compiler_params=SMALL,
        cost_estimate=CHEAP,
        name="prepare",
    )(in_hbm(green), coupling, earlier)


class Terms:
    def __init__(self, scalar_refs, factor_refs, scratch):
        self.lists, self.offsets, self.shifts, self.occupation = scalar_refs
        self.left, self.right = factor_refs
        self.half, self.held, self.sems = scratch
        self.transfers, self.listed = self.left.shape[0], self.left.shape[1]
        self.block = self.left.shape[2] // 2

    def entry(self, q, n, side):
        return self.lists[(q * self.listed + n) * 2 + side]

    def fetch(self, wanted, slot, pairs):
        for holds, *blocks in pairs:

            @pl.when(wanted & holds)
            def _():
                for i, ref in enumerate(blocks):
                    pltpu.make_async_copy(ref, self.held.at[slot, i], self.sems.at[slot, i]).start()

    def arrive(self, slot):
        for i in range(2):
            pltpu.make_async_copy(self.held.at[slot, i], self.held.at[slot, i], self.sems.at[slot, i]).wait()

    def mixed(self, q, slot, m):
        away = self.occupation[q] + jnp.where(odd() == 1, 0.0, 1.0)
        towards = self.occupation[q] + jnp.where(odd() == 1, 1.0, 0.0)
        here = pl.ds(pl.multiple_of(m * self.block, self.block), self.block)

        def part(p):
            a = self.held[slot, 0, p, here, :].astype(jnp.float32)
            b = self.held[slot, 1, p, here, :].astype(jnp.float32)
            return (away * a + towards * b).astype(jnp.bfloat16)

        return jnp.concatenate([part(0), part(1)], axis=0)

    def multiply(self, q, slot, emit):
        block = self.block
        for n in range(self.listed):
            rows = self.mixed(q, slot, self.entry(q, n, 1))
            product = jnp.dot(self.left[q, n], rows, preferred_element_type=jnp.float32).astype(jnp.bfloat16)
            target = pl.ds(pl.multiple_of(self.entry(q, n, 0) * block, block), block)
            for column in range(self.listed):
                for part in range(2):
                    self.half[column, target, pl.ds(part * block, block)] = product[
                        part * block : (part + 1) * block, column * block : (column + 1) * block
                    ]
        for n in range(self.listed):
            product = jnp.dot(self.half[self.entry(q, n, 1)], self.right[q, n], preferred_element_type=jnp.float32)
            emit(self.entry(q, n, 0), product)


def term_scratch(slots, coupling_shape, orbitals):
    _, listed, _, block, _ = coupling_shape
    return [
        pltpu.VMEM((listed, orbitals, 2 * block), jnp.bfloat16),
        pltpu.VMEM((slots, 2, 2, orbitals, orbitals), jnp.bfloat16),
        pltpu.SemaphoreType.DMA((slots, 2)),
    ]


def levels_of(chip_mate, *others):
    return (chip_mate.at[0, 1 - odd()], chip_mate.at[0, odd()], *others)


def at_row_end(row):
    place, count = lax.axis_index("en"), lax.axis_size("en")
    if count % row:
        return place < 0
    return (place % row == 0) | (place % row == row - 1)


def pairs_of(place, shift, levels, row=None):
    first, second = levels[place - shift + SMAX], levels[place + shift + SMAX]
    if row is None or place + shift != SMAX:
        return [(True, first, second)]
    return [(jnp.logical_not(at_row_end(row)), first, second), (at_row_end(row), first, levels[-1])]


def message_kernel(place, offset, row, *refs):
    terms = Terms(refs[:4], refs[4:6], refs[-3:])
    levels = levels_of(*refs[6:-5])
    message_ref, total = refs[-5:-3]
    for q in range(terms.transfers):
        for shift in range(1, SMAX + 1):
            wanted = (terms.offsets[q] == offset) & (terms.shifts[q] == shift)
            terms.fetch(wanted, q, pairs_of(place, shift, levels, row))
    total[...] = jnp.zeros_like(total)

    @pl.loop(0, terms.transfers)
    def _(q):
        @pl.when(terms.offsets[q] == offset)
        def _():
            def emit(column, product):
                total[column] += product

            terms.arrive(q)
            terms.multiply(q, q, emit)

    message_ref[...] = total[...].astype(jnp.bfloat16)


def add_to(total, place, block):
    def emit(column, product):
        columns = pl.ds(pl.multiple_of(column * block, block), block)
        for part in range(2):
            total[place, part, :, columns] += product[:, part * block : (part + 1) * block]

    return emit


def first_kernel(own_offset, near_offset, row, *refs):
    terms = Terms(refs[:4], refs[4:6], refs[-3:])
    own, near, totals = levels_of(*refs[6:12]), refs[12:17], refs[17]
    places = totals.shape[0]
    for q in range(terms.transfers):
        for place in range(places):
            for shift in range(1, SMAX + 1):
                slot, here = q * places + place, terms.shifts[q] == shift
                terms.fetch(here & (terms.offsets[q] == own_offset), slot, pairs_of(place, shift, own, row))
                if place + shift <= SMAX:
                    terms.fetch(here & (terms.offsets[q] == near_offset), slot, pairs_of(place, shift, near))
    totals[...] = jnp.zeros_like(totals)

    @pl.loop(0, terms.transfers * places)
    def _(slot):
        q = slot // places
        place = slot - q * places
        is_near = (terms.offsets[q] == near_offset) & (terms.shifts[q] + place <= SMAX)

        @pl.when((terms.offsets[q] == own_offset) | is_near)
        def _():
            terms.arrive(slot)
            terms.multiply(q, slot, add_to(totals, place, terms.block))


def second_kernel(near_offset, place, *refs):
    terms = Terms(refs[:4], refs[4:6], refs[-3:])
    first, second, sum_ref, total = refs[6:-3]

    def wanted(q):
        return (terms.offsets[q] == near_offset) & (terms.shifts[q] + place > SMAX)

    any_wanted = functools.reduce(jnp.logical_or, [wanted(q) for q in range(terms.transfers)])
    terms.fetch(any_wanted, 0, [(True, first, second)])
    total[0] = sum_ref[place]

    @pl.when(any_wanted)
    def _():
        terms.arrive(0)

    @pl.loop(0, terms.transfers)
    def _(q):
        @pl.when(wanted(q))
        def _():
            terms.multiply(q, 0, add_to(total, 0, terms.block))


def store_kernel(place, sum_ref, arrived_ref, *refs):
    out_ref, held, arrived, sems = refs[-4:]
    listed, orbitals, width = arrived.shape
    block = width // 2
    energy = odd() * place + (1 - odd()) * (1 - place)
    step = orbitals // sems.shape[1]
    rows = [pl.ds(piece * step, step) for piece in range(sems.shape[1])]

    def read(i):
        return pltpu.make_async_copy(arrived_ref.at[:, rows[i], :], arrived.at[:, rows[i], :], sems.at[0, i])

    def write(i):
        return pltpu.make_async_copy(held.at[:, rows[i], :], out_ref.at[0, energy, :, rows[i], :], sems.at[1, i])

    for i in range(len(rows)):
        read(i).start()
    for i, here in enumerate(rows):
        read(i).wait()
        for column in range(listed):
            columns = pl.ds(column * block, block)
            for part in range(2):
                held[part, here, columns] = sum_ref[0, part, here, columns] + arrived[
                    column, here, pl.ds(part * block, block)
                ].astype(jnp.float32)
        write(i).start()
    for i in range(len(rows)):
        write(i).wait()


def store(place, sums, arrived, result, *earlier):
    return pl.pallas_call(
        functools.partial(store_kernel, place),
        in_specs=[VMEM, ANY] + [ANY] * len(earlier),
        out_specs=ANY,
        out_shape=result,
        scratch_shapes=[
            pltpu.VMEM(result.shape[2:], jnp.float32),
            pltpu.VMEM(arrived.shape, arrived.dtype),
            pltpu.SemaphoreType.DMA((2, 2 * PIECES)),
        ],
        input_output_aliases={2: 0} if earlier else {},
        compiler_params=SMALL,
        cost_estimate=CHEAP,
        name="store%d" % place,
    )(in_vmem(sums), arrived, *earlier)


def on_device(green_lesser, coupling, block_list, offsets, shifts, occupation):
    _, energies, _, orbitals, _ = green_lesser.shape
    transfers, listed, _, block, _ = coupling.shape
    assert green_lesser.shape[0] == 1 and energies == SMAX
    momenta, ranks = lax.axis_size("kz"), lax.axis_size("en")
    forward, backward = ring(momenta, 1), ring(momenta, -1)
    scalar_args = (block_list.reshape(-1), offsets, shifts, occupation)
    result = jax.ShapeDtypeStruct(green_lesser.shape, jnp.float32)

    on_chip = both_ways([(i, i + 1) for i in range(0, ranks - 1, 2)])
    between = both_ways([(i, i + 1) for i in range(1, ranks - 1, 2)])
    row = 2 ** math.ceil(math.log2(ranks) / 2)
    turns = [i for i in range(row - 1, ranks - 1, row) if ranks % row == 0]
    across = [(i, j) for i, j in between if min(i, j) not in turns]
    across += [(i, i + row) for i in turns] + [(i + 1, i + 1 - row) for i in turns]
    arriving = [(i + row, i + 1) for i in turns] + [(i + 1 - row, i) for i in turns]

    def call(kernel, out_shape, slots, name, *operands, sums=(), scratch=()):
        return pl.pallas_call(
            kernel,
            in_specs=[SMEM] * 4 + [VMEM] * 2 + [ANY] * len(operands) + [VMEM] * len(sums),
            out_specs=VMEM,
            out_shape=out_shape,
            scratch_shapes=[*scratch, *term_scratch(slots, coupling.shape, orbitals)],
            compiler_params=LARGE,
            cost_estimate=CHEAP,
            name=name,
        )(*scalar_args, in_vmem(left), in_vmem(right), *operands, *[in_vmem(x) for x in sums])

    def message(place, *operands):
        total = pltpu.VMEM((listed, orbitals, 2 * block), jnp.float32)
        kernel = functools.partial(message_kernel, place, 1, row)
        return call(
            kernel,
            jax.ShapeDtypeStruct(total.shape, jnp.bfloat16),
            transfers,
            "message%d" % place,
            *operands,
            scratch=[total],
        )

    def sums_at(count):
        return pltpu.VMEM((count, *green_lesser.shape[2:]), jnp.float32)

    own1 = take(green_lesser)
    near1 = lax.ppermute(own1, "kz", backward)
    own2 = lax.ppermute(own1, "en", across)
    own0, left, right = prepare(green_lesser, coupling, own1)
    near0 = lax.ppermute(own0, "kz", backward)
    own3 = lax.ppermute(own0, "en", between)
    own_ = lax.ppermute(green_lesser, "en", on_chip)

    mate1 = lax.ppermute(near1, "en", on_chip)
    own_ = after(own_, near1)
    own2 = after(own2, near1)
    relayed2 = lax.ppermute(own2, "en", arriving)
    own = (own_, own0, own1, own2, own3, relayed2)
    sent0 = message(0, *own[:-2], relayed2)
    arrived0 = lax.ppermute(sent0, "kz", forward)
    near1 = after(near1, sent0, mate1)
    near2 = lax.ppermute(near1, "en", between)
    sent1 = message(1, *own)
    arrived1 = lax.ppermute(sent1, "kz", forward)
    near0 = after(near0, sent1, sent0, mate1)
    near3 = lax.ppermute(near0, "en", between)
    mate0 = lax.ppermute(near0, "en", on_chip)
    near2 = after(near2, arrived0)

    near = (mate1, mate0, near0, near1, near2)
    first = functools.partial(first_kernel, 0, -1, row)
    sums = call(first, sums_at(energies), transfers * energies, "first", *own, *near)
    partial = store(0, sums, arrived0, result)
    second = functools.partial(second_kernel, -1, 1)
    sums = call(second, sums_at(1), 1, "second", mate0, near3, sums=[sums])
    return store(1, sums, arrived1, result, partial)


def solution(mesh):
    placed = (P("kz", "en", None, None, None), P(), P(), P(), P(), P())
    return jax.shard_map(
        on_device,
        mesh=mesh,
        in_specs=placed,
        out_specs=P("kz", "en", None, None, None),
        check_vma=False,
    )
```

```python
import functools
import math

import jax
import jax.numpy as jnp
from jax import lax
from jax.experimental import pallas as pl
from jax.experimental.pallas import tpu as pltpu
from jax.sharding import PartitionSpec as P

SMAX = 2
PIECES = 4
MIB = 1024 * 1024
SMALL = pltpu.CompilerParams(vmem_limit_bytes=6 * MIB)
LARGE = pltpu.CompilerParams(vmem_limit_bytes=24 * MIB)
ANY = pl.BlockSpec(memory_space=pl.ANY)
SMEM = pl.BlockSpec(memory_space=pltpu.SMEM)
VMEM = pl.BlockSpec(memory_space=pltpu.VMEM)
DEAR = pl.CostEstimate(flops=2 * 10**11, bytes_accessed=1, transcendentals=0)
CHEAP = pl.CostEstimate(flops=1, bytes_accessed=1, transcendentals=0)


def ring(count, step):
    return [(i, (i + step) % count) for i in range(count)]


def both_ways(pairs):
    return [*pairs, *[(j, i) for i, j in pairs]]


def in_vmem(x):
    return pltpu.with_memory_space_constraint(x, pltpu.VMEM)


def in_hbm(x):
    return pltpu.with_memory_space_constraint(x, pltpu.HBM)


def after(value, *earlier, cost=DEAR):
    return pl.pallas_call(
        lambda *refs: None,
        in_specs=[ANY] * (1 + len(earlier)),
        out_specs=ANY,
        out_shape=jax.ShapeDtypeStruct(value.shape, value.dtype),
        input_output_aliases={0: 0},
        compiler_params=SMALL,
        cost_estimate=cost,
        name="after",
    )(value, *earlier)


def odd():
    return lax.axis_index("en") % 2


def pieces_of(ref, count):
    rows = ref.shape[-2] // count
    return [(part, pl.ds(piece * rows, rows)) for part in range(2) for piece in range(count)]


def carry(green_ref, energy, out_ref, held, sems):
    places = pieces_of(held, PIECES)

    def copy(i, way):
        part, here = places[i]
        ends = (green_ref.at[0, energy, part, here, :], held.at[part, here, :], out_ref.at[part, here, :])
        return pltpu.make_async_copy(ends[way], ends[way + 1], sems.at[way, i])

    for i in range(len(places)):
        copy(i, 0).start()

    def finish():
        for i in range(len(places)):
            copy(i, 0).wait()
            copy(i, 1).start()
        for i in range(len(places)):
            copy(i, 1).wait()

    return finish


def carry_scratch(green):
    return [pltpu.VMEM(green.shape[2:], green.dtype), pltpu.SemaphoreType.DMA((2, 2 * PIECES))]


def take_kernel(green_ref, out_ref, sems):
    copies = []
    for i, (part, here) in enumerate(pieces_of(out_ref, PIECES)):
        copies.append(
            pltpu.make_async_copy(green_ref.at[0, odd(), part, here, :], out_ref.at[part, here, :], sems.at[i])
        )
        copies[-1].start()
    for copy in copies:
        copy.wait()


def take(green):
    return pl.pallas_call(
        take_kernel,
        in_specs=[ANY],
        out_specs=VMEM,
        out_shape=pltpu.VMEM(green.shape[2:], green.dtype),
        scratch_shapes=[pltpu.SemaphoreType.DMA((2 * PIECES,))],
        compiler_params=SMALL,
        cost_estimate=CHEAP,
        name="take",
    )(in_hbm(green))


def prepare_kernel(green_ref, coupling_ref, _, out_ref, left_ref, right_ref, held, sems):
    finish = carry(green_ref, 1 - odd(), out_ref, held, sems)
    transfers, listed, _, block, _ = coupling_ref.shape
    low, high = pl.ds(0, block), pl.ds(block, block)

    @pl.loop(0, transfers)
    def _(q):
        for n in range(listed):
            real, imag = coupling_ref[q, n, 0], coupling_ref[q, n, 1]
            for ref, a, b in ((left_ref, real, imag), (right_ref, real.T, imag.T)):
                ref[q, n, low, low] = a.astype(jnp.bfloat16)
                ref[q, n, low, high] = (-b).astype(jnp.bfloat16)
                ref[q, n, high, low] = b.astype(jnp.bfloat16)
                ref[q, n, high, high] = a.astype(jnp.bfloat16)

    finish()


def prepare(green, coupling, earlier):
    transfers, listed, _, block, _ = coupling.shape
    factor = pltpu.VMEM((transfers, listed, 2 * block, 2 * block), jnp.bfloat16)
    return pl.pallas_call(
        prepare_kernel,
        in_specs=[ANY, VMEM, ANY],
        out_specs=[ANY, VMEM, VMEM],
        out_shape=[jax.ShapeDtypeStruct(green.shape[2:], green.dtype), factor, factor],
        scratch_shapes=carry_scratch(green),
        compiler_params=SMALL,
        cost_estimate=CHEAP,
        name="prepare",
    )(in_hbm(green), coupling, earlier)


class Terms:
    def __init__(self, scalar_refs, factor_refs, scratch):
        self.lists, self.offsets, self.shifts, self.occupation = scalar_refs
        self.left, self.right = factor_refs
        self.half, self.held, self.sems = scratch
        self.transfers, self.listed = self.left.shape[0], self.left.shape[1]
        self.block = self.left.shape[2] // 2

    def entry(self, q, n, side):
        return self.lists[(q * self.listed + n) * 2 + side]

    def fetch(self, wanted, slot, pairs):
        for holds, *blocks in pairs:

            @pl.when(wanted & holds)
            def _():
                for i, ref in enumerate(blocks):
                    pltpu.make_async_copy(ref, self.held.at[slot, i], self.sems.at[slot, i]).start()

    def arrive(self, slot):
        for i in range(2):
            pltpu.make_async_copy(self.held.at[slot, i], self.held.at[slot, i], self.sems.at[slot, i]).wait()

    def mixed(self, q, slot, m):
        away = self.occupation[q] + jnp.where(odd() == 1, 0.0, 1.0)
        towards = self.occupation[q] + jnp.where(odd() == 1, 1.0, 0.0)
        here = pl.ds(pl.multiple_of(m * self.block, self.block), self.block)

        def part(p):
            a = self.held[slot, 0, p, here, :].astype(jnp.float32)
            b = self.held[slot, 1, p, here, :].astype(jnp.float32)
            return (away * a + towards * b).astype(jnp.bfloat16)

        return jnp.concatenate([part(0), part(1)], axis=0)

    def multiply(self, q, slot, emit):
        block = self.block
        for n in range(self.listed):
            rows = self.mixed(q, slot, self.entry(q, n, 1))
            product = jnp.dot(self.left[q, n], rows, preferred_element_type=jnp.float32).astype(jnp.bfloat16)
            target = pl.ds(pl.multiple_of(self.entry(q, n, 0) * block, block), block)
            for column in range(self.listed):
                for part in range(2):
                    self.half[column, target, pl.ds(part * block, block)] = product[
                        part * block : (part + 1) * block, column * block : (column + 1) * block
                    ]
        for n in range(self.listed):
            product = jnp.dot(self.half[self.entry(q, n, 1)], self.right[q, n], preferred_element_type=jnp.float32)
            emit(self.entry(q, n, 0), product)


def term_scratch(slots, coupling_shape, orbitals):
    _, listed, _, block, _ = coupling_shape
    return [
        pltpu.VMEM((listed, orbitals, 2 * block), jnp.bfloat16),
        pltpu.VMEM((slots, 2, 2, orbitals, orbitals), jnp.bfloat16),
        pltpu.SemaphoreType.DMA((slots, 2)),
    ]


def levels_of(chip_mate, *others):
    return (chip_mate.at[0, 1 - odd()], chip_mate.at[0, odd()], *others)


def at_row_end(row):
    place, count = lax.axis_index("en"), lax.axis_size("en")
    if count % row:
        return place < 0
    return (place % row == 0) | (place % row == row - 1)


def pairs_of(place, shift, levels, row=None):
    first, second = levels[place - shift + SMAX], levels[place + shift + SMAX]
    if row is None or place + shift != SMAX:
        return [(True, first, second)]
    return [(jnp.logical_not(at_row_end(row)), first, second), (at_row_end(row), first, levels[-1])]


def message_kernel(place, offset, row, *refs):
    terms = Terms(refs[:4], refs[4:6], refs[-3:])
    levels = levels_of(*refs[6:-5])
    message_ref, total = refs[-5:-3]
    for q in range(terms.transfers):
        for shift in range(1, SMAX + 1):
            wanted = (terms.offsets[q] == offset) & (terms.shifts[q] == shift)
            terms.fetch(wanted, q, pairs_of(place, shift, levels, row))
    total[...] = jnp.zeros_like(total)

    @pl.loop(0, terms.transfers)
    def _(q):
        @pl.when(terms.offsets[q] == offset)
        def _():
            def emit(column, product):
                total[column] += product

            terms.arrive(q)
            terms.multiply(q, q, emit)

    message_ref[...] = total[...].astype(jnp.bfloat16)


def add_to(total, place, block):
    def emit(column, product):
        columns = pl.ds(pl.multiple_of(column * block, block), block)
        for part in range(2):
            total[place, part, :, columns] += product[:, part * block : (part + 1) * block]

    return emit


def first_kernel(own_offset, near_offset, row, *refs):
    terms = Terms(refs[:4], refs[4:6], refs[-3:])
    own, near, totals = levels_of(*refs[6:12]), refs[12:17], refs[17]
    places = totals.shape[0]
    for q in range(terms.transfers):
        for place in range(places):
            for shift in range(1, SMAX + 1):
                slot, here = q * places + place, terms.shifts[q] == shift
                terms.fetch(here & (terms.offsets[q] == own_offset), slot, pairs_of(place, shift, own, row))
                if place + shift <= SMAX:
                    terms.fetch(here & (terms.offsets[q] == near_offset), slot, pairs_of(place, shift, near))
    totals[...] = jnp.zeros_like(totals)

    @pl.loop(0, terms.transfers * places)
    def _(slot):
        q = slot // places
        place = slot - q * places
        is_near = (terms.offsets[q] == near_offset) & (terms.shifts[q] + place <= SMAX)

        @pl.when((terms.offsets[q] == own_offset) | is_near)
        def _():
            terms.arrive(slot)
            terms.multiply(q, slot, add_to(totals, place, terms.block))


def second_kernel(near_offset, place, *refs):
    terms = Terms(refs[:4], refs[4:6], refs[-3:])
    first, second, sum_ref, total = refs[6:-3]

    def wanted(q):
        return (terms.offsets[q] == near_offset) & (terms.shifts[q] + place > SMAX)

    any_wanted = functools.reduce(jnp.logical_or, [wanted(q) for q in range(terms.transfers)])
    terms.fetch(any_wanted, 0, [(True, first, second)])
    total[0] = sum_ref[place]

    @pl.when(any_wanted)
    def _():
        terms.arrive(0)

    @pl.loop(0, terms.transfers)
    def _(q):
        @pl.when(wanted(q))
        def _():
            terms.multiply(q, 0, add_to(total, 0, terms.block))


def store_kernel(place, sum_ref, arrived, *refs):
    out_ref, held, sems = refs[-3:]
    listed, orbitals, width = arrived.shape
    block = width // 2
    energy = odd() * place + (1 - odd()) * (1 - place)
    copies = []
    for piece in range(orbitals // block):
        rows = pl.ds(piece * block, block)
        for column in range(listed):
            columns = pl.ds(column * block, block)
            for part in range(2):
                held[part, rows, columns] = sum_ref[0, part, rows, columns] + arrived[
                    column, rows, pl.ds(part * block, block)
                ].astype(jnp.float32)
        copies.append(pltpu.make_async_copy(held.at[:, rows, :], out_ref.at[0, energy, :, rows, :], sems.at[piece]))
        copies[-1].start()
    for copy in copies:
        copy.wait()


def store(place, sums, arrived, result, *earlier):
    return pl.pallas_call(
        functools.partial(store_kernel, place),
        in_specs=[VMEM, VMEM] + [ANY] * len(earlier),
        out_specs=ANY,
        out_shape=result,
        scratch_shapes=[
            pltpu.VMEM(result.shape[2:], jnp.float32),
            pltpu.SemaphoreType.DMA((2 * arrived.shape[1] // arrived.shape[2],)),
        ],
        input_output_aliases={2: 0} if earlier else {},
        compiler_params=SMALL,
        cost_estimate=CHEAP,
        name="store%d" % place,
    )(in_vmem(sums), in_vmem(arrived), *earlier)


def on_device(green_lesser, coupling, block_list, offsets, shifts, occupation):
    _, energies, _, orbitals, _ = green_lesser.shape
    transfers, listed, _, block, _ = coupling.shape
    assert green_lesser.shape[0] == 1 and energies == SMAX
    momenta, ranks = lax.axis_size("kz"), lax.axis_size("en")
    forward, backward = ring(momenta, 1), ring(momenta, -1)
    scalar_args = (block_list.reshape(-1), offsets, shifts, occupation)
    result = jax.ShapeDtypeStruct(green_lesser.shape, jnp.float32)

    on_chip = both_ways([(i, i + 1) for i in range(0, ranks - 1, 2)])
    between = both_ways([(i, i + 1) for i in range(1, ranks - 1, 2)])
    row = 2 ** math.ceil(math.log2(ranks) / 2)
    turns = [i for i in range(row - 1, ranks - 1, row) if ranks % row == 0]
    across = [(i, j) for i, j in between if min(i, j) not in turns]
    across += [(i, i + row) for i in turns] + [(i + 1, i + 1 - row) for i in turns]
    arriving = [(i + row, i + 1) for i in turns] + [(i + 1 - row, i) for i in turns]

    def call(kernel, out_shape, slots, name, *operands, sums=(), scratch=()):
        return pl.pallas_call(
            kernel,
            in_specs=[SMEM] * 4 + [VMEM] * 2 + [ANY] * len(operands) + [VMEM] * len(sums),
            out_specs=VMEM,
            out_shape=out_shape,
            scratch_shapes=[*scratch, *term_scratch(slots, coupling.shape, orbitals)],
            compiler_params=LARGE,
            cost_estimate=CHEAP,
            name=name,
        )(*scalar_args, in_vmem(left), in_vmem(right), *operands, *[in_vmem(x) for x in sums])

    def message(place, *operands):
        total = pltpu.VMEM((listed, orbitals, 2 * block), jnp.float32)
        kernel = functools.partial(message_kernel, place, 1, row)
        return call(
            kernel,
            pltpu.VMEM(total.shape, jnp.bfloat16),
            transfers,
            "message%d" % place,
            *operands,
            scratch=[total],
        )

    def sums_at(count):
        return pltpu.VMEM((count, *green_lesser.shape[2:]), jnp.float32)

    own1 = take(green_lesser)
    near1 = lax.ppermute(own1, "kz", backward)
    own2 = lax.ppermute(own1, "en", across)
    own0, left, right = prepare(green_lesser, coupling, own1)
    near0 = lax.ppermute(own0, "kz", backward)
    own3 = lax.ppermute(own0, "en", between)
    own_ = lax.ppermute(green_lesser, "en", on_chip)

    mate1 = lax.ppermute(near1, "en", on_chip)
    own_ = after(own_, near1)
    own2 = after(own2, near1)
    relayed2 = lax.ppermute(own2, "en", arriving)
    own = (own_, own0, own1, own2, own3, relayed2)
    sent0 = message(0, *own[:-2], relayed2)
    arrived0 = lax.ppermute(sent0, "kz", forward)
    near1 = after(near1, sent0, mate1, cost=CHEAP)
    near2 = lax.ppermute(near1, "en", between)
    sent1 = message(1, *own)
    arrived1 = lax.ppermute(sent1, "kz", forward)
    near0 = after(near0, sent1, sent0, mate1, cost=CHEAP)
    near3 = lax.ppermute(near0, "en", between)
    mate0 = lax.ppermute(near0, "en", on_chip)
    near2 = after(near2, arrived0, cost=CHEAP)

    near = (mate1, mate0, near0, near1, near2)
    first = functools.partial(first_kernel, 0, -1, row)
    sums = call(first, sums_at(energies), transfers * energies, "first", *own, *near)
    partial = store(0, sums, arrived0, result)
    second = functools.partial(second_kernel, -1, 1)
    sums = call(second, sums_at(1), 1, "second", mate0, near3, sums=[sums])
    return store(1, sums, arrived1, result, partial)


def solution(mesh):
    placed = (P("kz", "en", None, None, None), P(), P(), P(), P(), P())
    return jax.shard_map(
        on_device,
        mesh=mesh,
        in_specs=placed,
        out_specs=P("kz", "en", None, None, None),
        check_vma=False,
    )
```

```python
import functools
import math

import jax
import jax.numpy as jnp
from jax import lax
from jax.experimental import pallas as pl
from jax.experimental.pallas import tpu as pltpu
from jax.sharding import PartitionSpec as P

SMAX = 2
PIECES = 1
MIB = 1024 * 1024
SMALL = pltpu.CompilerParams(vmem_limit_bytes=6 * MIB)
LARGE = pltpu.CompilerParams(vmem_limit_bytes=24 * MIB)
ANY = pl.BlockSpec(memory_space=pl.ANY)
SMEM = pl.BlockSpec(memory_space=pltpu.SMEM)
VMEM = pl.BlockSpec(memory_space=pltpu.VMEM)
DEAR = pl.CostEstimate(flops=2 * 10**11, bytes_accessed=1, transcendentals=0)
CHEAP = pl.CostEstimate(flops=1, bytes_accessed=1, transcendentals=0)


def ring(count, step):
    return [(i, (i + step) % count) for i in range(count)]


def both_ways(pairs):
    return [*pairs, *[(j, i) for i, j in pairs]]


def in_vmem(x):
    return pltpu.with_memory_space_constraint(x, pltpu.VMEM)


def in_hbm(x):
    return pltpu.with_memory_space_constraint(x, pltpu.HBM)


def after(value, *earlier, cost=DEAR):
    return pl.pallas_call(
        lambda *refs: None,
        in_specs=[ANY] * (1 + len(earlier)),
        out_specs=ANY,
        out_shape=jax.ShapeDtypeStruct(value.shape, value.dtype),
        input_output_aliases={0: 0},
        compiler_params=SMALL,
        cost_estimate=cost,
        name="after",
    )(value, *earlier)


def odd():
    return lax.axis_index("en") % 2


def pieces_of(ref, count):
    rows = ref.shape[-2] // count
    return [(part, pl.ds(piece * rows, rows)) for part in range(2) for piece in range(count)]


def carry(green_ref, energy, out_ref, held, sems):
    places = pieces_of(held, PIECES)

    def copy(i, way):
        part, here = places[i]
        ends = (green_ref.at[0, energy, part, here, :], held.at[part, here, :], out_ref.at[part, here, :])
        return pltpu.make_async_copy(ends[way], ends[way + 1], sems.at[way, i])

    for i in range(len(places)):
        copy(i, 0).start()

    def finish():
        for i in range(len(places)):
            copy(i, 0).wait()
            copy(i, 1).start()
        for i in range(len(places)):
            copy(i, 1).wait()

    return finish


def carry_scratch(green):
    return [pltpu.VMEM(green.shape[2:], green.dtype), pltpu.SemaphoreType.DMA((2, 2 * PIECES))]


def take_kernel(green_ref, out_ref, sems):
    copies = []
    for i, (part, here) in enumerate(pieces_of(out_ref, PIECES)):
        copies.append(
            pltpu.make_async_copy(green_ref.at[0, odd(), part, here, :], out_ref.at[part, here, :], sems.at[i])
        )
        copies[-1].start()
    for copy in copies:
        copy.wait()


def take(green):
    return pl.pallas_call(
        take_kernel,
        in_specs=[ANY],
        out_specs=VMEM,
        out_shape=pltpu.VMEM(green.shape[2:], green.dtype),
        scratch_shapes=[pltpu.SemaphoreType.DMA((2 * PIECES,))],
        compiler_params=SMALL,
        cost_estimate=CHEAP,
        name="take",
    )(in_hbm(green))


def prepare_kernel(green_ref, coupling_ref, _, out_ref, left_ref, right_ref, held, sems):
    finish = carry(green_ref, 1 - odd(), out_ref, held, sems)
    transfers, listed, _, block, _ = coupling_ref.shape
    low, high = pl.ds(0, block), pl.ds(block, block)

    @pl.loop(0, transfers)
    def _(q):
        for n in range(listed):
            real, imag = coupling_ref[q, n, 0], coupling_ref[q, n, 1]
            for ref, a, b in ((left_ref, real, imag), (right_ref, real.T, imag.T)):
                ref[q, n, low, low] = a.astype(jnp.bfloat16)
                ref[q, n, low, high] = (-b).astype(jnp.bfloat16)
                ref[q, n, high, low] = b.astype(jnp.bfloat16)
                ref[q, n, high, high] = a.astype(jnp.bfloat16)

    finish()


def prepare(green, coupling, earlier):
    transfers, listed, _, block, _ = coupling.shape
    factor = pltpu.VMEM((transfers, listed, 2 * block, 2 * block), jnp.bfloat16)
    return pl.pallas_call(
        prepare_kernel,
        in_specs=[ANY, VMEM, ANY],
        out_specs=[ANY, VMEM, VMEM],
        out_shape=[jax.ShapeDtypeStruct(green.shape[2:], green.dtype), factor, factor],
        scratch_shapes=carry_scratch(green),
        compiler_params=SMALL,
        cost_estimate=CHEAP,
        name="prepare",
    )(in_hbm(green), coupling, earlier)


class Terms:
    def __init__(self, scalar_refs, factor_refs, scratch):
        self.lists, self.offsets, self.shifts, self.occupation = scalar_refs
        self.left, self.right = factor_refs
        self.half, self.held, self.sems = scratch
        self.transfers, self.listed = self.left.shape[0], self.left.shape[1]
        self.block = self.left.shape[2] // 2

    def entry(self, q, n, side):
        return self.lists[(q * self.listed + n) * 2 + side]

    def fetch(self, wanted, slot, pairs):
        for holds, *blocks in pairs:

            @pl.when(wanted & holds)
            def _():
                for i, ref in enumerate(blocks):
                    pltpu.make_async_copy(ref, self.held.at[slot, i], self.sems.at[slot, i]).start()

    def arrive(self, slot):
        for i in range(2):
            pltpu.make_async_copy(self.held.at[slot, i], self.held.at[slot, i], self.sems.at[slot, i]).wait()

    def mixed(self, q, slot, m):
        away = self.occupation[q] + jnp.where(odd() == 1, 0.0, 1.0)
        towards = self.occupation[q] + jnp.where(odd() == 1, 1.0, 0.0)
        here = pl.ds(pl.multiple_of(m * self.block, self.block), self.block)

        def part(p):
            a = self.held[slot, 0, p, here, :].astype(jnp.float32)
            b = self.held[slot, 1, p, here, :].astype(jnp.float32)
            return (away * a + towards * b).astype(jnp.bfloat16)

        return jnp.concatenate([part(0), part(1)], axis=0)

    def multiply(self, q, slot, emit):
        block = self.block
        for n in range(self.listed):
            rows = self.mixed(q, slot, self.entry(q, n, 1))
            product = jnp.dot(self.left[q, n], rows, preferred_element_type=jnp.float32).astype(jnp.bfloat16)
            target = pl.ds(pl.multiple_of(self.entry(q, n, 0) * block, block), block)
            for column in range(self.listed):
                for part in range(2):
                    self.half[column, target, pl.ds(part * block, block)] = product[
                        part * block : (part + 1) * block, column * block : (column + 1) * block
                    ]
        for n in range(self.listed):
            product = jnp.dot(self.half[self.entry(q, n, 1)], self.right[q, n], preferred_element_type=jnp.float32)
            emit(self.entry(q, n, 0), product)


def term_scratch(slots, coupling_shape, orbitals):
    _, listed, _, block, _ = coupling_shape
    return [
        pltpu.VMEM((listed, orbitals, 2 * block), jnp.bfloat16),
        pltpu.VMEM((slots, 2, 2, orbitals, orbitals), jnp.bfloat16),
        pltpu.SemaphoreType.DMA((slots, 2)),
    ]


def levels_of(chip_mate, *others):
    return (chip_mate.at[0, 1 - odd()], chip_mate.at[0, odd()], *others)


def at_row_end(row):
    place, count = lax.axis_index("en"), lax.axis_size("en")
    if count % row:
        return place < 0
    return (place % row == 0) | (place % row == row - 1)


def pairs_of(place, shift, levels, row=None):
    first, second = levels[place - shift + SMAX], levels[place + shift + SMAX]
    if row is None or place + shift != SMAX:
        return [(True, first, second)]
    return [(jnp.logical_not(at_row_end(row)), first, second), (at_row_end(row), first, levels[-1])]


def message_kernel(place, offset, row, *refs):
    terms = Terms(refs[:4], refs[4:6], refs[-3:])
    levels = levels_of(*refs[6:-5])
    message_ref, total = refs[-5:-3]
    for q in range(terms.transfers):
        for shift in range(1, SMAX + 1):
            wanted = (terms.offsets[q] == offset) & (terms.shifts[q] == shift)
            terms.fetch(wanted, q, pairs_of(place, shift, levels, row))
    total[...] = jnp.zeros_like(total)

    @pl.loop(0, terms.transfers)
    def _(q):
        @pl.when(terms.offsets[q] == offset)
        def _():
            def emit(column, product):
                total[column] += product

            terms.arrive(q)
            terms.multiply(q, q, emit)

    message_ref[...] = total[...].astype(jnp.bfloat16)


def add_to(total, place, block):
    def emit(column, product):
        columns = pl.ds(pl.multiple_of(column * block, block), block)
        for part in range(2):
            total[place, part, :, columns] += product[:, part * block : (part + 1) * block]

    return emit


def first_kernel(own_offset, near_offset, row, *refs):
    terms = Terms(refs[:4], refs[4:6], refs[-3:])
    own, near, totals = levels_of(*refs[6:12]), refs[12:17], refs[17]
    places = totals.shape[0]
    for q in range(terms.transfers):
        for place in range(places):
            for shift in range(1, SMAX + 1):
                slot, here = q * places + place, terms.shifts[q] == shift
                terms.fetch(here & (terms.offsets[q] == own_offset), slot, pairs_of(place, shift, own, row))
                if place + shift <= SMAX:
                    terms.fetch(here & (terms.offsets[q] == near_offset), slot, pairs_of(place, shift, near))
    totals[...] = jnp.zeros_like(totals)

    @pl.loop(0, terms.transfers * places)
    def _(slot):
        q = slot // places
        place = slot - q * places
        is_near = (terms.offsets[q] == near_offset) & (terms.shifts[q] + place <= SMAX)

        @pl.when((terms.offsets[q] == own_offset) | is_near)
        def _():
            terms.arrive(slot)
            terms.multiply(q, slot, add_to(totals, place, terms.block))


def second_kernel(near_offset, place, *refs):
    terms = Terms(refs[:4], refs[4:6], refs[-3:])
    first, second, sum_ref, total = refs[6:-3]

    def wanted(q):
        return (terms.offsets[q] == near_offset) & (terms.shifts[q] + place > SMAX)

    any_wanted = functools.reduce(jnp.logical_or, [wanted(q) for q in range(terms.transfers)])
    terms.fetch(any_wanted, 0, [(True, first, second)])
    total[0] = sum_ref[place]

    @pl.when(any_wanted)
    def _():
        terms.arrive(0)

    @pl.loop(0, terms.transfers)
    def _(q):
        @pl.when(wanted(q))
        def _():
            terms.multiply(q, 0, add_to(total, 0, terms.block))


def store_kernel(place, sum_ref, arrived, *refs):
    out_ref, held, sems = refs[-3:]
    listed, orbitals, width = arrived.shape
    block = width // 2
    energy = odd() * place + (1 - odd()) * (1 - place)
    copies = []
    for piece in range(orbitals // block):
        rows = pl.ds(piece * block, block)
        for column in range(listed):
            columns = pl.ds(column * block, block)
            for part in range(2):
                held[part, rows, columns] = sum_ref[0, part, rows, columns] + arrived[
                    column, rows, pl.ds(part * block, block)
                ].astype(jnp.float32)
        copies.append(pltpu.make_async_copy(held.at[:, rows, :], out_ref.at[0, energy, :, rows, :], sems.at[piece]))
        copies[-1].start()
    for copy in copies:
        copy.wait()


def store(place, sums, arrived, result, *earlier):
    return pl.pallas_call(
        functools.partial(store_kernel, place),
        in_specs=[VMEM, VMEM] + [ANY] * len(earlier),
        out_specs=ANY,
        out_shape=result,
        scratch_shapes=[
            pltpu.VMEM(result.shape[2:], jnp.float32),
            pltpu.SemaphoreType.DMA((2 * arrived.shape[1] // arrived.shape[2],)),
        ],
        input_output_aliases={2: 0} if earlier else {},
        compiler_params=SMALL,
        cost_estimate=CHEAP,
        name="store%d" % place,
    )(in_vmem(sums), in_vmem(arrived), *earlier)


def on_device(green_lesser, coupling, block_list, offsets, shifts, occupation):
    _, energies, _, orbitals, _ = green_lesser.shape
    transfers, listed, _, block, _ = coupling.shape
    assert green_lesser.shape[0] == 1 and energies == SMAX
    momenta, ranks = lax.axis_size("kz"), lax.axis_size("en")
    forward, backward = ring(momenta, 1), ring(momenta, -1)
    scalar_args = (block_list.reshape(-1), offsets, shifts, occupation)
    result = jax.ShapeDtypeStruct(green_lesser.shape, jnp.float32)

    on_chip = both_ways([(i, i + 1) for i in range(0, ranks - 1, 2)])
    between = both_ways([(i, i + 1) for i in range(1, ranks - 1, 2)])
    row = 2 ** math.ceil(math.log2(ranks) / 2)
    turns = [i for i in range(row - 1, ranks - 1, row) if ranks % row == 0]
    across = [(i, j) for i, j in between if min(i, j) not in turns]
    across += [(i, i + row) for i in turns] + [(i + 1, i + 1 - row) for i in turns]
    arriving = [(i + row, i + 1) for i in turns] + [(i + 1 - row, i) for i in turns]

    def call(kernel, out_shape, slots, name, *operands, sums=(), scratch=()):
        return pl.pallas_call(
            kernel,
            in_specs=[SMEM] * 4 + [VMEM] * 2 + [ANY] * len(operands) + [VMEM] * len(sums),
            out_specs=VMEM,
            out_shape=out_shape,
            scratch_shapes=[*scratch, *term_scratch(slots, coupling.shape, orbitals)],
            compiler_params=LARGE,
            cost_estimate=CHEAP,
            name=name,
        )(*scalar_args, in_vmem(left), in_vmem(right), *operands, *[in_vmem(x) for x in sums])

    def message(place, *operands):
        total = pltpu.VMEM((listed, orbitals, 2 * block), jnp.float32)
        kernel = functools.partial(message_kernel, place, 1, row)
        return call(
            kernel,
            pltpu.VMEM(total.shape, jnp.bfloat16),
            transfers,
            "message%d" % place,
            *operands,
            scratch=[total],
        )

    def sums_at(count):
        return pltpu.VMEM((count, *green_lesser.shape[2:]), jnp.float32)

    own1 = take(green_lesser)
    near1 = lax.ppermute(own1, "kz", backward)
    own2 = lax.ppermute(own1, "en", across)
    own0, left, right = prepare(green_lesser, coupling, own1)
    near0 = lax.ppermute(own0, "kz", backward)
    own3 = lax.ppermute(own0, "en", between)
    own_ = lax.ppermute(green_lesser, "en", on_chip)

    mate1 = lax.ppermute(near1, "en", on_chip)
    own_ = after(own_, near1)
    own2 = after(own2, near1)
    relayed2 = lax.ppermute(own2, "en", arriving)
    own = (own_, own0, own1, own2, own3, relayed2)
    sent0 = message(0, *own[:-2], relayed2)
    arrived0 = lax.ppermute(sent0, "kz", forward)
    near1 = after(near1, sent0, mate1, cost=CHEAP)
    near2 = lax.ppermute(near1, "en", between)
    sent1 = message(1, *own)
    arrived1 = lax.ppermute(sent1, "kz", forward)
    near0 = after(near0, sent1, sent0, mate1, cost=CHEAP)
    near3 = lax.ppermute(near0, "en", between)
    mate0 = lax.ppermute(near0, "en", on_chip)
    near2 = after(near2, arrived0, cost=CHEAP)

    near = (mate1, mate0, near0, near1, near2)
    first = functools.partial(first_kernel, 0, -1, row)
    sums = call(first, sums_at(energies), transfers * energies, "first", *own, *near)
    partial = store(0, sums, arrived0, result)
    second = functools.partial(second_kernel, -1, 1)
    sums = call(second, sums_at(1), 1, "second", mate0, near3, sums=[sums])
    return store(1, sums, arrived1, result, partial)


def solution(mesh):
    placed = (P("kz", "en", None, None, None), P(), P(), P(), P(), P())
    return jax.shard_map(
        on_device,
        mesh=mesh,
        in_specs=placed,
        out_specs=P("kz", "en", None, None, None),
        check_vma=False,
    )
```

```python
import functools
import math

import jax
import jax.numpy as jnp
from jax import lax
from jax.experimental import pallas as pl
from jax.experimental.pallas import tpu as pltpu
from jax.sharding import PartitionSpec as P

SMAX = 2
PIECES = 1
MIB = 1024 * 1024
SMALL = pltpu.CompilerParams(vmem_limit_bytes=6 * MIB)
LARGE = pltpu.CompilerParams(vmem_limit_bytes=24 * MIB)
ANY = pl.BlockSpec(memory_space=pl.ANY)
SMEM = pl.BlockSpec(memory_space=pltpu.SMEM)
VMEM = pl.BlockSpec(memory_space=pltpu.VMEM)
DEAR = pl.CostEstimate(flops=2 * 10**11, bytes_accessed=1, transcendentals=0)
CHEAP = pl.CostEstimate(flops=1, bytes_accessed=1, transcendentals=0)


def ring(count, step):
    return [(i, (i + step) % count) for i in range(count)]


def both_ways(pairs):
    return [*pairs, *[(j, i) for i, j in pairs]]


def in_vmem(x):
    return pltpu.with_memory_space_constraint(x, pltpu.VMEM)


def in_hbm(x):
    return pltpu.with_memory_space_constraint(x, pltpu.HBM)


def after(value, *earlier, cost=DEAR):
    return pl.pallas_call(
        lambda *refs: None,
        in_specs=[ANY] * (1 + len(earlier)),
        out_specs=ANY,
        out_shape=jax.ShapeDtypeStruct(value.shape, value.dtype),
        input_output_aliases={0: 0},
        compiler_params=SMALL,
        cost_estimate=cost,
        name="after",
    )(value, *earlier)


def odd():
    return lax.axis_index("en") % 2


def pieces_of(ref, count):
    rows = ref.shape[-2] // count
    return [(part, pl.ds(piece * rows, rows)) for part in range(2) for piece in range(count)]


def carry(green_ref, energy, out_ref, held, sems):
    places = pieces_of(held, PIECES)

    def copy(i, way):
        part, here = places[i]
        ends = (green_ref.at[0, energy, part, here, :], held.at[part, here, :], out_ref.at[part, here, :])
        return pltpu.make_async_copy(ends[way], ends[way + 1], sems.at[way, i])

    for i in range(len(places)):
        copy(i, 0).start()

    def finish():
        for i in range(len(places)):
            copy(i, 0).wait()
            copy(i, 1).start()
        for i in range(len(places)):
            copy(i, 1).wait()

    return finish


def carry_scratch(green):
    return [pltpu.VMEM(green.shape[2:], green.dtype), pltpu.SemaphoreType.DMA((2, 2 * PIECES))]


def take_kernel(green_ref, out_ref, sems):
    copies = []
    for i, (part, here) in enumerate(pieces_of(out_ref, PIECES)):
        copies.append(
            pltpu.make_async_copy(green_ref.at[0, odd(), part, here, :], out_ref.at[part, here, :], sems.at[i])
        )
        copies[-1].start()
    for copy in copies:
        copy.wait()


def take(green):
    return pl.pallas_call(
        take_kernel,
        in_specs=[ANY],
        out_specs=VMEM,
        out_shape=pltpu.VMEM(green.shape[2:], green.dtype),
        scratch_shapes=[pltpu.SemaphoreType.DMA((2 * PIECES,))],
        compiler_params=SMALL,
        cost_estimate=CHEAP,
        name="take",
    )(in_hbm(green))


def prepare_kernel(green_ref, coupling_ref, _, out_ref, left_ref, right_ref, held, sems):
    finish = carry(green_ref, 1 - odd(), out_ref, held, sems)
    transfers, listed, _, block, _ = coupling_ref.shape
    low, high = pl.ds(0, block), pl.ds(block, block)

    @pl.loop(0, transfers)
    def _(q):
        for n in range(listed):
            real, imag = coupling_ref[q, n, 0], coupling_ref[q, n, 1]
            for ref, a, b in ((left_ref, real, imag), (right_ref, real.T, imag.T)):
                ref[q, n, low, low] = a.astype(jnp.bfloat16)
                ref[q, n, low, high] = (-b).astype(jnp.bfloat16)
                ref[q, n, high, low] = b.astype(jnp.bfloat16)
                ref[q, n, high, high] = a.astype(jnp.bfloat16)

    finish()


def prepare(green, coupling, earlier):
    transfers, listed, _, block, _ = coupling.shape
    factor = pltpu.VMEM((transfers, listed, 2 * block, 2 * block), jnp.bfloat16)
    return pl.pallas_call(
        prepare_kernel,
        in_specs=[ANY, VMEM, ANY],
        out_specs=[ANY, VMEM, VMEM],
        out_shape=[jax.ShapeDtypeStruct(green.shape[2:], green.dtype), factor, factor],
        scratch_shapes=carry_scratch(green),
        compiler_params=SMALL,
        cost_estimate=CHEAP,
        name="prepare",
    )(in_hbm(green), coupling, earlier)


class Terms:
    def __init__(self, scalar_refs, factor_refs, scratch):
        self.lists, self.offsets, self.shifts, self.occupation = scalar_refs
        self.left, self.right = factor_refs
        self.half, self.held, self.sems = scratch
        self.transfers, self.listed = self.left.shape[0], self.left.shape[1]
        self.block = self.left.shape[2] // 2

    def entry(self, q, n, side):
        return self.lists[(q * self.listed + n) * 2 + side]

    def fetch(self, wanted, slot, pairs):
        for holds, *blocks in pairs:

            @pl.when(wanted & holds)
            def _():
                for i, ref in enumerate(blocks):
                    pltpu.make_async_copy(ref, self.held.at[slot, i], self.sems.at[slot, i]).start()

    def arrive(self, slot):
        for i in range(2):
            pltpu.make_async_copy(self.held.at[slot, i], self.held.at[slot, i], self.sems.at[slot, i]).wait()

    def mixed(self, q, slot, m):
        away = self.occupation[q] + jnp.where(odd() == 1, 0.0, 1.0)
        towards = self.occupation[q] + jnp.where(odd() == 1, 1.0, 0.0)
        here = pl.ds(pl.multiple_of(m * self.block, self.block), self.block)

        def part(p):
            a = self.held[slot, 0, p, here, :].astype(jnp.float32)
            b = self.held[slot, 1, p, here, :].astype(jnp.float32)
            return (away * a + towards * b).astype(jnp.bfloat16)

        return jnp.concatenate([part(0), part(1)], axis=0)

    def multiply(self, q, slot, emit):
        block = self.block
        for n in range(self.listed):
            rows = self.mixed(q, slot, self.entry(q, n, 1))
            product = jnp.dot(self.left[q, n], rows, preferred_element_type=jnp.float32).astype(jnp.bfloat16)
            target = pl.ds(pl.multiple_of(self.entry(q, n, 0) * block, block), block)
            for column in range(self.listed):
                for part in range(2):
                    self.half[column, target, pl.ds(part * block, block)] = product[
                        part * block : (part + 1) * block, column * block : (column + 1) * block
                    ]
        for n in range(self.listed):
            product = jnp.dot(self.half[self.entry(q, n, 1)], self.right[q, n], preferred_element_type=jnp.float32)
            emit(self.entry(q, n, 0), product)


def term_scratch(slots, coupling_shape, orbitals):
    _, listed, _, block, _ = coupling_shape
    return [
        pltpu.VMEM((listed, orbitals, 2 * block), jnp.bfloat16),
        pltpu.VMEM((slots, 2, 2, orbitals, orbitals), jnp.bfloat16),
        pltpu.SemaphoreType.DMA((slots, 2)),
    ]


def levels_of(chip_mate, *others):
    return (chip_mate.at[0, 1 - odd()], chip_mate.at[0, odd()], *others)


def at_row_end(row):
    place, count = lax.axis_index("en"), lax.axis_size("en")
    if count % row:
        return place < 0
    return (place % row == 0) | (place % row == row - 1)


def pairs_of(place, shift, levels, row=None):
    first, second = levels[place - shift + SMAX], levels[place + shift + SMAX]
    if row is None or place + shift != SMAX:
        return [(True, first, second)]
    return [(jnp.logical_not(at_row_end(row)), first, second), (at_row_end(row), first, levels[-1])]


def message_kernel(place, offset, row, count, *refs):
    terms = Terms(refs[:4], refs[4:6], refs[-3:])
    levels = levels_of(*refs[6 : -4 - count])
    message_refs, total = refs[-4 - count : -4], refs[-4]
    for q in range(terms.transfers):
        for shift in range(1, SMAX + 1):
            wanted = (terms.offsets[q] == offset) & (terms.shifts[q] == shift)
            terms.fetch(wanted, q, pairs_of(place, shift, levels, row))
    total[...] = jnp.zeros_like(total)

    @pl.loop(0, terms.transfers)
    def _(q):
        @pl.when(terms.offsets[q] == offset)
        def _():
            def emit(column, product):
                total[column] += product

            terms.arrive(q)
            terms.multiply(q, q, emit)

    for i, ref in enumerate(message_refs):
        ref[...] = total[:, pl.ds(i * ref.shape[1], ref.shape[1]), :].astype(jnp.bfloat16)


def add_to(total, place, block):
    def emit(column, product):
        columns = pl.ds(pl.multiple_of(column * block, block), block)
        for part in range(2):
            total[place, part, :, columns] += product[:, part * block : (part + 1) * block]

    return emit


def first_kernel(own_offset, near_offset, row, *refs):
    terms = Terms(refs[:4], refs[4:6], refs[-3:])
    own, near, totals = levels_of(*refs[6:12]), refs[12:17], refs[17]
    places = totals.shape[0]
    for q in range(terms.transfers):
        for place in range(places):
            for shift in range(1, SMAX + 1):
                slot, here = q * places + place, terms.shifts[q] == shift
                terms.fetch(here & (terms.offsets[q] == own_offset), slot, pairs_of(place, shift, own, row))
                if place + shift <= SMAX:
                    terms.fetch(here & (terms.offsets[q] == near_offset), slot, pairs_of(place, shift, near))
    totals[...] = jnp.zeros_like(totals)

    @pl.loop(0, terms.transfers * places)
    def _(slot):
        q = slot // places
        place = slot - q * places
        is_near = (terms.offsets[q] == near_offset) & (terms.shifts[q] + place <= SMAX)

        @pl.when((terms.offsets[q] == own_offset) | is_near)
        def _():
            terms.arrive(slot)
            terms.multiply(q, slot, add_to(totals, place, terms.block))


def second_kernel(near_offset, place, *refs):
    terms = Terms(refs[:4], refs[4:6], refs[-3:])
    first, second, sum_ref, total = refs[6:-3]

    def wanted(q):
        return (terms.offsets[q] == near_offset) & (terms.shifts[q] + place > SMAX)

    any_wanted = functools.reduce(jnp.logical_or, [wanted(q) for q in range(terms.transfers)])
    terms.fetch(any_wanted, 0, [(True, first, second)])
    total[0] = sum_ref[place]

    @pl.when(any_wanted)
    def _():
        terms.arrive(0)

    @pl.loop(0, terms.transfers)
    def _(q):
        @pl.when(wanted(q))
        def _():
            terms.multiply(q, 0, add_to(total, 0, terms.block))


def store_kernel(place, start, sum_ref, arrived, *refs):
    out_ref, held, sems = refs[-3:]
    listed, count, width = arrived.shape
    block = width // 2
    energy = odd() * place + (1 - odd()) * (1 - place)
    copies = []
    for piece in range(count // block):
        here, rows = pl.ds(piece * block, block), pl.ds(start + piece * block, block)
        for column in range(listed):
            columns = pl.ds(column * block, block)
            for part in range(2):
                held[part, rows, columns] = sum_ref[0, part, rows, columns] + arrived[
                    column, here, pl.ds(part * block, block)
                ].astype(jnp.float32)
        copies.append(pltpu.make_async_copy(held.at[:, rows, :], out_ref.at[0, energy, :, rows, :], sems.at[piece]))
        copies[-1].start()
    for copy in copies:
        copy.wait()


def store(place, sums, arrived, result, *earlier, half=0):
    return pl.pallas_call(
        functools.partial(store_kernel, place, half * arrived.shape[1]),
        in_specs=[VMEM, VMEM] + [ANY] * len(earlier),
        out_specs=ANY,
        out_shape=result,
        scratch_shapes=[
            pltpu.VMEM(result.shape[2:], jnp.float32),
            pltpu.SemaphoreType.DMA((2 * arrived.shape[1] // arrived.shape[2],)),
        ],
        input_output_aliases={2: 0} if earlier else {},
        compiler_params=SMALL,
        cost_estimate=CHEAP,
        name="store%d%d" % (place, half),
    )(in_vmem(sums), in_vmem(arrived), *earlier)


def on_device(green_lesser, coupling, block_list, offsets, shifts, occupation):
    _, energies, _, orbitals, _ = green_lesser.shape
    transfers, listed, _, block, _ = coupling.shape
    assert green_lesser.shape[0] == 1 and energies == SMAX
    momenta, ranks = lax.axis_size("kz"), lax.axis_size("en")
    forward, backward = ring(momenta, 1), ring(momenta, -1)
    scalar_args = (block_list.reshape(-1), offsets, shifts, occupation)
    result = jax.ShapeDtypeStruct(green_lesser.shape, jnp.float32)

    on_chip = both_ways([(i, i + 1) for i in range(0, ranks - 1, 2)])
    between = both_ways([(i, i + 1) for i in range(1, ranks - 1, 2)])
    row = 2 ** math.ceil(math.log2(ranks) / 2)
    turns = [i for i in range(row - 1, ranks - 1, row) if ranks % row == 0]
    across = [(i, j) for i, j in between if min(i, j) not in turns]
    across += [(i, i + row) for i in turns] + [(i + 1, i + 1 - row) for i in turns]
    arriving = [(i + row, i + 1) for i in turns] + [(i + 1 - row, i) for i in turns]

    def call(kernel, out_shape, slots, name, *operands, sums=(), scratch=()):
        return pl.pallas_call(
            kernel,
            in_specs=[SMEM] * 4 + [VMEM] * 2 + [ANY] * len(operands) + [VMEM] * len(sums),
            out_specs=[VMEM] * len(out_shape) if isinstance(out_shape, list) else VMEM,
            out_shape=out_shape,
            scratch_shapes=[*scratch, *term_scratch(slots, coupling.shape, orbitals)],
            compiler_params=LARGE,
            cost_estimate=CHEAP,
            name=name,
        )(*scalar_args, in_vmem(left), in_vmem(right), *operands, *[in_vmem(x) for x in sums])

    def message(place, count, *operands):
        total = pltpu.VMEM((listed, orbitals, 2 * block), jnp.float32)
        kernel = functools.partial(message_kernel, place, 1, row, count)
        return call(
            kernel,
            [pltpu.VMEM((listed, orbitals // count, 2 * block), jnp.bfloat16)] * count,
            transfers,
            "message%d" % place,
            *operands,
            scratch=[total],
        )

    def sums_at(count):
        return pltpu.VMEM((count, *green_lesser.shape[2:]), jnp.float32)

    own1 = take(green_lesser)
    near1 = lax.ppermute(own1, "kz", backward)
    own2 = lax.ppermute(own1, "en", across)
    own0, left, right = prepare(green_lesser, coupling, own1)
    near0 = lax.ppermute(own0, "kz", backward)
    own3 = lax.ppermute(own0, "en", between)
    own_ = lax.ppermute(green_lesser, "en", on_chip)

    mate1 = lax.ppermute(near1, "en", on_chip)
    own_ = after(own_, near1)
    own2 = after(own2, near1)
    relayed2 = lax.ppermute(own2, "en", arriving)
    own = (own_, own0, own1, own2, own3, relayed2)
    (sent0,) = message(0, 1, *own[:-2], relayed2)
    arrived0 = lax.ppermute(sent0, "kz", forward)
    near1 = after(near1, sent0, mate1, cost=CHEAP)
    near2 = lax.ppermute(near1, "en", between)
    sent1, sent2 = message(1, 2, *own)
    arrived1 = lax.ppermute(sent1, "kz", forward)
    arrived2 = lax.ppermute(sent2, "kz", forward)
    near0 = after(near0, sent1, sent0, mate1, cost=CHEAP)
    near3 = lax.ppermute(near0, "en", between)
    mate0 = lax.ppermute(near0, "en", on_chip)
    near2 = after(near2, arrived0, cost=CHEAP)

    near = (mate1, mate0, near0, near1, near2)
    first = functools.partial(first_kernel, 0, -1, row)
    sums = call(first, sums_at(energies), transfers * energies, "first", *own, *near)
    partial = store(0, sums, arrived0, result)
    second = functools.partial(second_kernel, -1, 1)
    sums = call(second, sums_at(1), 1, "second", mate0, near3, sums=[sums])
    partial = store(1, sums, arrived1, result, partial)
    return store(1, sums, arrived2, result, partial, half=1)


def solution(mesh):
    placed = (P("kz", "en", None, None, None), P(), P(), P(), P(), P())
    return jax.shard_map(
        on_device,
        mesh=mesh,
        in_specs=placed,
        out_specs=P("kz", "en", None, None, None),
        check_vma=False,
    )
```

```python
import functools
import math

import jax
import jax.numpy as jnp
from jax import lax
from jax.experimental import pallas as pl
from jax.experimental.pallas import tpu as pltpu
from jax.sharding import PartitionSpec as P

SMAX = 2
PIECES = 1
MIB = 1024 * 1024
SMALL = pltpu.CompilerParams(vmem_limit_bytes=6 * MIB)
LARGE = pltpu.CompilerParams(vmem_limit_bytes=24 * MIB)
ANY = pl.BlockSpec(memory_space=pl.ANY)
SMEM = pl.BlockSpec(memory_space=pltpu.SMEM)
VMEM = pl.BlockSpec(memory_space=pltpu.VMEM)
DEAR = pl.CostEstimate(flops=2 * 10**11, bytes_accessed=1, transcendentals=0)
CHEAP = pl.CostEstimate(flops=1, bytes_accessed=1, transcendentals=0)


def ring(count, step):
    return [(i, (i + step) % count) for i in range(count)]


def both_ways(pairs):
    return [*pairs, *[(j, i) for i, j in pairs]]


def in_vmem(x):
    return pltpu.with_memory_space_constraint(x, pltpu.VMEM)


def in_hbm(x):
    return pltpu.with_memory_space_constraint(x, pltpu.HBM)


def after(value, *earlier, cost=DEAR):
    return pl.pallas_call(
        lambda *refs: None,
        in_specs=[ANY] * (1 + len(earlier)),
        out_specs=ANY,
        out_shape=jax.ShapeDtypeStruct(value.shape, value.dtype),
        input_output_aliases={0: 0},
        compiler_params=SMALL,
        cost_estimate=cost,
        name="after",
    )(value, *earlier)


def odd():
    return lax.axis_index("en") % 2


def pieces_of(ref, count):
    rows = ref.shape[-2] // count
    return [(part, pl.ds(piece * rows, rows)) for part in range(2) for piece in range(count)]


def carry(green_ref, energy, out_ref, held, sems):
    places = pieces_of(held, PIECES)

    def copy(i, way):
        part, here = places[i]
        ends = (green_ref.at[0, energy, part, here, :], held.at[part, here, :], out_ref.at[part, here, :])
        return pltpu.make_async_copy(ends[way], ends[way + 1], sems.at[way, i])

    for i in range(len(places)):
        copy(i, 0).start()

    def finish():
        for i in range(len(places)):
            copy(i, 0).wait()
            copy(i, 1).start()
        for i in range(len(places)):
            copy(i, 1).wait()

    return finish


def carry_scratch(green):
    return [pltpu.VMEM(green.shape[2:], green.dtype), pltpu.SemaphoreType.DMA((2, 2 * PIECES))]


def take_kernel(green_ref, out_ref, sem):
    copy = pltpu.make_async_copy(green_ref.at[0, odd()], out_ref, sem)
    copy.start()
    copy.wait()


def take(green):
    return pl.pallas_call(
        take_kernel,
        in_specs=[ANY],
        out_specs=VMEM,
        out_shape=pltpu.VMEM(green.shape[2:], green.dtype),
        scratch_shapes=[pltpu.SemaphoreType.DMA],
        compiler_params=SMALL,
        cost_estimate=CHEAP,
        name="take",
    )(in_hbm(green))


def prepare_kernel(green_ref, coupling_ref, _, out_ref, left_ref, right_ref, held, sems):
    finish = carry(green_ref, 1 - odd(), out_ref, held, sems)
    transfers, listed, _, block, _ = coupling_ref.shape
    low, high = pl.ds(0, block), pl.ds(block, block)

    @pl.loop(0, transfers)
    def _(q):
        for n in range(listed):
            real, imag = coupling_ref[q, n, 0], coupling_ref[q, n, 1]
            for ref, a, b in ((left_ref, real, imag), (right_ref, real.T, imag.T)):
                ref[q, n, low, low] = a.astype(jnp.bfloat16)
                ref[q, n, low, high] = (-b).astype(jnp.bfloat16)
                ref[q, n, high, low] = b.astype(jnp.bfloat16)
                ref[q, n, high, high] = a.astype(jnp.bfloat16)

    finish()


def prepare(green, coupling, earlier):
    transfers, listed, _, block, _ = coupling.shape
    factor = pltpu.VMEM((transfers, listed, 2 * block, 2 * block), jnp.bfloat16)
    return pl.pallas_call(
        prepare_kernel,
        in_specs=[ANY, VMEM, ANY],
        out_specs=[ANY, VMEM, VMEM],
        out_shape=[jax.ShapeDtypeStruct(green.shape[2:], green.dtype), factor, factor],
        scratch_shapes=carry_scratch(green),
        compiler_params=SMALL,
        cost_estimate=CHEAP,
        name="prepare",
    )(in_hbm(green), coupling, earlier)


class Terms:
    def __init__(self, scalar_refs, factor_refs, scratch):
        self.lists, self.offsets, self.shifts, self.occupation = scalar_refs
        self.left, self.right = factor_refs
        self.half, self.held, self.sems = scratch
        self.transfers, self.listed = self.left.shape[0], self.left.shape[1]
        self.block = self.left.shape[2] // 2

    def entry(self, q, n, side):
        return self.lists[(q * self.listed + n) * 2 + side]

    def fetch(self, wanted, slot, pairs):
        for holds, *blocks in pairs:

            @pl.when(wanted & holds)
            def _():
                for i, ref in enumerate(blocks):
                    pltpu.make_async_copy(ref, self.held.at[slot, i], self.sems.at[slot, i]).start()

    def arrive(self, slot):
        for i in range(2):
            pltpu.make_async_copy(self.held.at[slot, i], self.held.at[slot, i], self.sems.at[slot, i]).wait()

    def mixed(self, q, slot, m):
        away = self.occupation[q] + jnp.where(odd() == 1, 0.0, 1.0)
        towards = self.occupation[q] + jnp.where(odd() == 1, 1.0, 0.0)
        here = pl.ds(pl.multiple_of(m * self.block, self.block), self.block)

        def part(p):
            a = self.held[slot, 0, p, here, :].astype(jnp.float32)
            b = self.held[slot, 1, p, here, :].astype(jnp.float32)
            return (away * a + towards * b).astype(jnp.bfloat16)

        return jnp.concatenate([part(0), part(1)], axis=0)

    def multiply(self, q, slot, emit):
        block = self.block
        for n in range(self.listed):
            rows = self.mixed(q, slot, self.entry(q, n, 1))
            product = jnp.dot(self.left[q, n], rows, preferred_element_type=jnp.float32).astype(jnp.bfloat16)
            target = pl.ds(pl.multiple_of(self.entry(q, n, 0) * block, block), block)
            for column in range(self.listed):
                for part in range(2):
                    self.half[column, target, pl.ds(part * block, block)] = product[
                        part * block : (part + 1) * block, column * block : (column + 1) * block
                    ]
        for n in range(self.listed):
            product = jnp.dot(self.half[self.entry(q, n, 1)], self.right[q, n], preferred_element_type=jnp.float32)
            emit(self.entry(q, n, 0), product)


def term_scratch(slots, coupling_shape, orbitals):
    _, listed, _, block, _ = coupling_shape
    return [
        pltpu.VMEM((listed, orbitals, 2 * block), jnp.bfloat16),
        pltpu.VMEM((slots, 2, 2, orbitals, orbitals), jnp.bfloat16),
        pltpu.SemaphoreType.DMA((slots, 2)),
    ]


def levels_of(chip_mate, *others):
    return (chip_mate.at[0, 1 - odd()], chip_mate.at[0, odd()], *others)


def at_row_end(row):
    place, count = lax.axis_index("en"), lax.axis_size("en")
    if count % row:
        return place < 0
    return (place % row == 0) | (place % row == row - 1)


def pairs_of(place, shift, levels, row=None):
    first, second = levels[place - shift + SMAX], levels[place + shift + SMAX]
    if row is None or place + shift != SMAX:
        return [(True, first, second)]
    return [(jnp.logical_not(at_row_end(row)), first, second), (at_row_end(row), first, levels[-1])]


def message_kernel(place, offset, row, count, *refs):
    terms = Terms(refs[:4], refs[4:6], refs[-3:])
    levels = levels_of(*refs[6 : -4 - count])
    message_refs, total = refs[-4 - count : -4], refs[-4]
    for q in range(terms.transfers):
        for shift in range(1, SMAX + 1):
            wanted = (terms.offsets[q] == offset) & (terms.shifts[q] == shift)
            terms.fetch(wanted, q, pairs_of(place, shift, levels, row))
    total[...] = jnp.zeros_like(total)

    @pl.loop(0, terms.transfers)
    def _(q):
        @pl.when(terms.offsets[q] == offset)
        def _():
            def emit(column, product):
                total[column] += product

            terms.arrive(q)
            terms.multiply(q, q, emit)

    for i, ref in enumerate(message_refs):
        ref[...] = total[:, pl.ds(i * ref.shape[1], ref.shape[1]), :].astype(jnp.bfloat16)


def add_to(total, place, block):
    def emit(column, product):
        columns = pl.ds(pl.multiple_of(column * block, block), block)
        for part in range(2):
            total[place, part, :, columns] += product[:, part * block : (part + 1) * block]

    return emit


def first_kernel(own_offset, near_offset, row, *refs):
    terms = Terms(refs[:4], refs[4:6], refs[-3:])
    own, near, totals = levels_of(*refs[6:12]), refs[12:17], refs[17]
    places = totals.shape[0]
    for q in range(terms.transfers):
        for place in range(places):
            for shift in range(1, SMAX + 1):
                slot, here = q * places + place, terms.shifts[q] == shift
                terms.fetch(here & (terms.offsets[q] == own_offset), slot, pairs_of(place, shift, own, row))
                if place + shift <= SMAX:
                    terms.fetch(here & (terms.offsets[q] == near_offset), slot, pairs_of(place, shift, near))
    totals[...] = jnp.zeros_like(totals)

    @pl.loop(0, terms.transfers * places)
    def _(slot):
        q = slot // places
        place = slot - q * places
        is_near = (terms.offsets[q] == near_offset) & (terms.shifts[q] + place <= SMAX)

        @pl.when((terms.offsets[q] == own_offset) | is_near)
        def _():
            terms.arrive(slot)
            terms.multiply(q, slot, add_to(totals, place, terms.block))


def second_kernel(near_offset, place, *refs):
    terms = Terms(refs[:4], refs[4:6], refs[-3:])
    first, second, sum_ref, total = refs[6:-3]

    def wanted(q):
        return (terms.offsets[q] == near_offset) & (terms.shifts[q] + place > SMAX)

    any_wanted = functools.reduce(jnp.logical_or, [wanted(q) for q in range(terms.transfers)])
    terms.fetch(any_wanted, 0, [(True, first, second)])
    total[0] = sum_ref[place]

    @pl.when(any_wanted)
    def _():
        terms.arrive(0)

    @pl.loop(0, terms.transfers)
    def _(q):
        @pl.when(wanted(q))
        def _():
            terms.multiply(q, 0, add_to(total, 0, terms.block))


def store_kernel(place, start, sum_ref, arrived, *refs):
    out_ref, held, sems = refs[-3:]
    listed, count, width = arrived.shape
    block = width // 2
    energy = odd() * place + (1 - odd()) * (1 - place)
    copies = []
    for piece in range(count // block):
        here, rows = pl.ds(piece * block, block), pl.ds(start + piece * block, block)
        for column in range(listed):
            columns = pl.ds(column * block, block)
            for part in range(2):
                held[part, rows, columns] = sum_ref[0, part, rows, columns] + arrived[
                    column, here, pl.ds(part * block, block)
                ].astype(jnp.float32)
        copies.append(pltpu.make_async_copy(held.at[:, rows, :], out_ref.at[0, energy, :, rows, :], sems.at[piece]))
        copies[-1].start()
    for copy in copies:
        copy.wait()


def store(place, sums, arrived, result, *earlier, half=0):
    return pl.pallas_call(
        functools.partial(store_kernel, place, half * arrived.shape[1]),
        in_specs=[VMEM, VMEM] + [ANY] * len(earlier),
        out_specs=ANY,
        out_shape=result,
        scratch_shapes=[
            pltpu.VMEM(result.shape[2:], jnp.float32),
            pltpu.SemaphoreType.DMA((2 * arrived.shape[1] // arrived.shape[2],)),
        ],
        input_output_aliases={2: 0} if earlier else {},
        compiler_params=SMALL,
        cost_estimate=CHEAP,
        name="store%d%d" % (place, half),
    )(in_vmem(sums), in_vmem(arrived), *earlier)


def on_device(green_lesser, coupling, block_list, offsets, shifts, occupation):
    _, energies, _, orbitals, _ = green_lesser.shape
    transfers, listed, _, block, _ = coupling.shape
    assert green_lesser.shape[0] == 1 and energies == SMAX
    momenta, ranks = lax.axis_size("kz"), lax.axis_size("en")
    forward, backward = ring(momenta, 1), ring(momenta, -1)
    scalar_args = (block_list.reshape(-1), offsets, shifts, occupation)
    result = jax.ShapeDtypeStruct(green_lesser.shape, jnp.float32)

    on_chip = both_ways([(i, i + 1) for i in range(0, ranks - 1, 2)])
    between = both_ways([(i, i + 1) for i in range(1, ranks - 1, 2)])
    row = 2 ** math.ceil(math.log2(ranks) / 2)
    turns = [i for i in range(row - 1, ranks - 1, row) if ranks % row == 0]
    across = [(i, j) for i, j in between if min(i, j) not in turns]
    across += [(i, i + row) for i in turns] + [(i + 1, i + 1 - row) for i in turns]
    arriving = [(i + row, i + 1) for i in turns] + [(i + 1 - row, i) for i in turns]

    def call(kernel, out_shape, slots, name, *operands, sums=(), scratch=()):
        return pl.pallas_call(
            kernel,
            in_specs=[SMEM] * 4 + [VMEM] * 2 + [ANY] * len(operands) + [VMEM] * len(sums),
            out_specs=[VMEM] * len(out_shape) if isinstance(out_shape, list) else VMEM,
            out_shape=out_shape,
            scratch_shapes=[*scratch, *term_scratch(slots, coupling.shape, orbitals)],
            compiler_params=LARGE,
            cost_estimate=CHEAP,
            name=name,
        )(*scalar_args, in_vmem(left), in_vmem(right), *operands, *[in_vmem(x) for x in sums])

    def message(place, count, *operands):
        total = pltpu.VMEM((listed, orbitals, 2 * block), jnp.float32)
        kernel = functools.partial(message_kernel, place, 1, row, count)
        return call(
            kernel,
            [pltpu.VMEM((listed, orbitals // count, 2 * block), jnp.bfloat16)] * count,
            transfers,
            "message%d" % place,
            *operands,
            scratch=[total],
        )

    def sums_at(count):
        return pltpu.VMEM((count, *green_lesser.shape[2:]), jnp.float32)

    own1 = take(green_lesser)
    near1 = lax.ppermute(own1, "kz", backward)
    own2 = lax.ppermute(own1, "en", across)
    own0, left, right = prepare(green_lesser, coupling, own1)
    near0 = lax.ppermute(own0, "kz", backward)
    own3 = lax.ppermute(own0, "en", between)
    own_ = lax.ppermute(green_lesser, "en", on_chip)

    mate1 = lax.ppermute(near1, "en", on_chip)
    own_ = after(own_, near1)
    own2 = after(own2, near1)
    relayed2 = lax.ppermute(own2, "en", arriving)
    own = (own_, own0, own1, own2, own3, relayed2)
    (sent0,) = message(0, 1, *own[:-2], relayed2)
    arrived0 = lax.ppermute(sent0, "kz", forward)
    near1 = after(near1, sent0, mate1, cost=CHEAP)
    near2 = lax.ppermute(near1, "en", between)
    sent1, sent2 = message(1, 2, *own)
    arrived1 = lax.ppermute(sent1, "kz", forward)
    arrived2 = lax.ppermute(sent2, "kz", forward)
    near0 = after(near0, sent1, sent0, mate1, cost=CHEAP)
    near3 = lax.ppermute(near0, "en", between)
    mate0 = lax.ppermute(near0, "en", on_chip)
    near2 = after(near2, arrived0, cost=CHEAP)

    near = (mate1, mate0, near0, near1, near2)
    first = functools.partial(first_kernel, 0, -1, row)
    sums = call(first, sums_at(energies), transfers * energies, "first", *own, *near)
    partial = store(0, sums, arrived0, result)
    second = functools.partial(second_kernel, -1, 1)
    sums = call(second, sums_at(1), 1, "second", mate0, near3, sums=[sums])
    partial = store(1, sums, arrived1, result, partial)
    return store(1, sums, arrived2, result, partial, half=1)


def solution(mesh):
    placed = (P("kz", "en", None, None, None), P(), P(), P(), P(), P())
    return jax.shard_map(
        on_device,
        mesh=mesh,
        in_specs=placed,
        out_specs=P("kz", "en", None, None, None),
        check_vma=False,
    )
```

```python
import functools
import math

import jax
import jax.numpy as jnp
from jax import lax
from jax.experimental import pallas as pl
from jax.experimental.pallas import tpu as pltpu
from jax.sharding import PartitionSpec as P

SMAX = 2
PIECES = 1
MIB = 1024 * 1024
SMALL = pltpu.CompilerParams(vmem_limit_bytes=6 * MIB)
LARGE = pltpu.CompilerParams(vmem_limit_bytes=24 * MIB)
ANY = pl.BlockSpec(memory_space=pl.ANY)
SMEM = pl.BlockSpec(memory_space=pltpu.SMEM)
VMEM = pl.BlockSpec(memory_space=pltpu.VMEM)
DEAR = pl.CostEstimate(flops=2 * 10**11, bytes_accessed=1, transcendentals=0)
CHEAP = pl.CostEstimate(flops=1, bytes_accessed=1, transcendentals=0)


def ring(count, step):
    return [(i, (i + step) % count) for i in range(count)]


def both_ways(pairs):
    return [*pairs, *[(j, i) for i, j in pairs]]


def in_vmem(x):
    return pltpu.with_memory_space_constraint(x, pltpu.VMEM)


def in_hbm(x):
    return pltpu.with_memory_space_constraint(x, pltpu.HBM)


def after(value, *earlier, cost=DEAR):
    return pl.pallas_call(
        lambda *refs: None,
        in_specs=[ANY] * (1 + len(earlier)),
        out_specs=ANY,
        out_shape=jax.ShapeDtypeStruct(value.shape, value.dtype),
        input_output_aliases={0: 0},
        compiler_params=SMALL,
        cost_estimate=cost,
        name="after",
    )(value, *earlier)


def odd():
    return lax.axis_index("en") % 2


def pieces_of(ref, count):
    rows = ref.shape[-2] // count
    return [(part, pl.ds(piece * rows, rows)) for part in range(2) for piece in range(count)]


def carry(green_ref, energy, out_ref, held, sems):
    places = pieces_of(held, PIECES)

    def copy(i, way):
        part, here = places[i]
        ends = (green_ref.at[0, energy, part, here, :], held.at[part, here, :], out_ref.at[part, here, :])
        return pltpu.make_async_copy(ends[way], ends[way + 1], sems.at[way, i])

    for i in range(len(places)):
        copy(i, 0).start()

    def finish():
        for i in range(len(places)):
            copy(i, 0).wait()
            copy(i, 1).start()
        for i in range(len(places)):
            copy(i, 1).wait()

    return finish


def carry_scratch(green):
    return [pltpu.VMEM(green.shape[2:], green.dtype), pltpu.SemaphoreType.DMA((2, 2 * PIECES))]


def take_kernel(green_ref, out_ref, sem):
    copy = pltpu.make_async_copy(green_ref.at[0, odd()], out_ref, sem)
    copy.start()
    copy.wait()


def take(green):
    return pl.pallas_call(
        take_kernel,
        in_specs=[ANY],
        out_specs=VMEM,
        out_shape=pltpu.VMEM(green.shape[2:], green.dtype),
        scratch_shapes=[pltpu.SemaphoreType.DMA],
        compiler_params=SMALL,
        cost_estimate=CHEAP,
        name="take",
    )(in_hbm(green))


def prepare_kernel(green_ref, coupling_ref, _, out_ref, left_ref, right_ref, held, sems):
    finish = carry(green_ref, 1 - odd(), out_ref, held, sems)
    transfers, listed, _, block, _ = coupling_ref.shape
    low, high = pl.ds(0, block), pl.ds(block, block)

    @pl.loop(0, transfers)
    def _(q):
        for n in range(listed):
            real, imag = coupling_ref[q, n, 0], coupling_ref[q, n, 1]
            for ref, a, b in ((left_ref, real, imag), (right_ref, real.T, imag.T)):
                ref[q, n, low, low] = a.astype(jnp.bfloat16)
                ref[q, n, low, high] = (-b).astype(jnp.bfloat16)
                ref[q, n, high, low] = b.astype(jnp.bfloat16)
                ref[q, n, high, high] = a.astype(jnp.bfloat16)

    finish()


def prepare(green, coupling, earlier):
    transfers, listed, _, block, _ = coupling.shape
    factor = pltpu.VMEM((transfers, listed, 2 * block, 2 * block), jnp.bfloat16)
    return pl.pallas_call(
        prepare_kernel,
        in_specs=[ANY, VMEM, ANY],
        out_specs=[ANY, VMEM, VMEM],
        out_shape=[jax.ShapeDtypeStruct(green.shape[2:], green.dtype), factor, factor],
        scratch_shapes=carry_scratch(green),
        compiler_params=SMALL,
        cost_estimate=CHEAP,
        name="prepare",
    )(in_hbm(green), coupling, earlier)


class Terms:
    def __init__(self, scalar_refs, factor_refs, scratch):
        self.lists, self.offsets, self.shifts, self.occupation = scalar_refs
        self.left, self.right = factor_refs
        self.half, self.held, self.sems = scratch
        self.transfers, self.listed = self.left.shape[0], self.left.shape[1]
        self.block = self.left.shape[2] // 2

    def entry(self, q, n, side):
        return self.lists[(q * self.listed + n) * 2 + side]

    def fetch(self, wanted, slot, pairs):
        for holds, *blocks in pairs:

            @pl.when(wanted & holds)
            def _():
                for i, ref in enumerate(blocks):
                    pltpu.make_async_copy(ref, self.held.at[slot, i], self.sems.at[slot, i]).start()

    def arrive(self, slot):
        for i in range(2):
            pltpu.make_async_copy(self.held.at[slot, i], self.held.at[slot, i], self.sems.at[slot, i]).wait()

    def mixed(self, q, slot, m):
        away = self.occupation[q] + jnp.where(odd() == 1, 0.0, 1.0)
        towards = self.occupation[q] + jnp.where(odd() == 1, 1.0, 0.0)
        here = pl.ds(pl.multiple_of(m * self.block, self.block), self.block)

        def part(p):
            a = self.held[slot, 0, p, here, :].astype(jnp.float32)
            b = self.held[slot, 1, p, here, :].astype(jnp.float32)
            return (away * a + towards * b).astype(jnp.bfloat16)

        return jnp.concatenate([part(0), part(1)], axis=0)

    def multiply(self, q, slot, emit):
        block = self.block
        for n in range(self.listed):
            rows = self.mixed(q, slot, self.entry(q, n, 1))
            product = jnp.dot(self.left[q, n], rows, preferred_element_type=jnp.float32).astype(jnp.bfloat16)
            target = pl.ds(pl.multiple_of(self.entry(q, n, 0) * block, block), block)
            for column in range(self.listed):
                for part in range(2):
                    self.half[column, target, pl.ds(part * block, block)] = product[
                        part * block : (part + 1) * block, column * block : (column + 1) * block
                    ]
        for n in range(self.listed):
            product = jnp.dot(self.half[self.entry(q, n, 1)], self.right[q, n], preferred_element_type=jnp.float32)
            emit(self.entry(q, n, 0), product)


def term_scratch(slots, coupling_shape, orbitals):
    _, listed, _, block, _ = coupling_shape
    return [
        pltpu.VMEM((listed, orbitals, 2 * block), jnp.bfloat16),
        pltpu.VMEM((slots, 2, 2, orbitals, orbitals), jnp.bfloat16),
        pltpu.SemaphoreType.DMA((slots, 2)),
    ]


def levels_of(chip_mate, *others):
    return (chip_mate.at[0, 1 - odd()], chip_mate.at[0, odd()], *others)


def at_row_end(row):
    place, count = lax.axis_index("en"), lax.axis_size("en")
    if count % row:
        return place < 0
    return (place % row == 0) | (place % row == row - 1)


def pairs_of(place, shift, levels, row=None):
    first, second = levels[place - shift + SMAX], levels[place + shift + SMAX]
    if row is None or place + shift != SMAX:
        return [(True, first, second)]
    return [(jnp.logical_not(at_row_end(row)), first, second), (at_row_end(row), first, levels[-1])]


def message_kernel(place, offset, row, count, *refs):
    terms = Terms(refs[:4], refs[4:6], refs[-3:])
    levels = levels_of(*refs[6 : -4 - count])
    message_refs, total = refs[-4 - count : -4], refs[-4]
    for q in range(terms.transfers):
        for shift in range(1, SMAX + 1):
            wanted = (terms.offsets[q] == offset) & (terms.shifts[q] == shift)
            terms.fetch(wanted, q, pairs_of(place, shift, levels, row))
    total[...] = jnp.zeros_like(total)

    @pl.loop(0, terms.transfers)
    def _(q):
        @pl.when(terms.offsets[q] == offset)
        def _():
            def emit(column, product):
                total[column] += product

            terms.arrive(q)
            terms.multiply(q, q, emit)

    for i, ref in enumerate(message_refs):
        ref[...] = total[:, pl.ds(i * ref.shape[1], ref.shape[1]), :].astype(jnp.bfloat16)


def add_to(total, place, block):
    def emit(column, product):
        columns = pl.ds(pl.multiple_of(column * block, block), block)
        for part in range(2):
            total[place, part, :, columns] += product[:, part * block : (part + 1) * block]

    return emit


def first_kernel(own_offset, near_offset, row, *refs):
    terms = Terms(refs[:4], refs[4:6], refs[-3:])
    own, near, totals = levels_of(*refs[6:12]), refs[12:17], refs[17]
    places = totals.shape[0]
    for q in range(terms.transfers):
        for place in range(places):
            for shift in range(1, SMAX + 1):
                slot, here = q * places + place, terms.shifts[q] == shift
                terms.fetch(here & (terms.offsets[q] == own_offset), slot, pairs_of(place, shift, own, row))
                if place + shift <= SMAX:
                    terms.fetch(here & (terms.offsets[q] == near_offset), slot, pairs_of(place, shift, near))
    totals[...] = jnp.zeros_like(totals)

    @pl.loop(0, terms.transfers * places)
    def _(slot):
        q = slot // places
        place = slot - q * places
        is_near = (terms.offsets[q] == near_offset) & (terms.shifts[q] + place <= SMAX)

        @pl.when((terms.offsets[q] == own_offset) | is_near)
        def _():
            terms.arrive(slot)
            terms.multiply(q, slot, add_to(totals, place, terms.block))


def second_kernel(near_offset, place, *refs):
    terms = Terms(refs[:4], refs[4:6], refs[-3:])
    first, second, sum_ref, total = refs[6:-3]

    def wanted(q):
        return (terms.offsets[q] == near_offset) & (terms.shifts[q] + place > SMAX)

    any_wanted = functools.reduce(jnp.logical_or, [wanted(q) for q in range(terms.transfers)])
    terms.fetch(any_wanted, 0, [(True, first, second)])
    total[0] = sum_ref[place]

    @pl.when(any_wanted)
    def _():
        terms.arrive(0)

    @pl.loop(0, terms.transfers)
    def _(q):
        @pl.when(wanted(q))
        def _():
            terms.multiply(q, 0, add_to(total, 0, terms.block))


def store_kernel(place, start, sum_ref, arrived, *refs):
    out_ref, held, sems = refs[-3:]
    listed, count, width = arrived.shape
    block = width // 2
    energy = odd() * place + (1 - odd()) * (1 - place)
    copies = []
    step = count // sems.shape[0]
    for piece in range(sems.shape[0]):
        here, rows = pl.ds(piece * step, step), pl.ds(start + piece * step, step)
        for column in range(listed):
            columns = pl.ds(column * block, block)
            for part in range(2):
                held[part, rows, columns] = sum_ref[0, part, rows, columns] + arrived[
                    column, here, pl.ds(part * block, block)
                ].astype(jnp.float32)
        copies.append(pltpu.make_async_copy(held.at[:, rows, :], out_ref.at[0, energy, :, rows, :], sems.at[piece]))
        copies[-1].start()
    for copy in copies:
        copy.wait()


def store(place, sums, arrived, result, *earlier, half=0):
    return pl.pallas_call(
        functools.partial(store_kernel, place, half * arrived.shape[1]),
        in_specs=[VMEM, VMEM] + [ANY] * len(earlier),
        out_specs=ANY,
        out_shape=result,
        scratch_shapes=[
            pltpu.VMEM(result.shape[2:], jnp.float32),
            pltpu.SemaphoreType.DMA((4,)),
        ],
        input_output_aliases={2: 0} if earlier else {},
        compiler_params=SMALL,
        cost_estimate=CHEAP,
        name="store%d%d" % (place, half),
    )(in_vmem(sums), in_vmem(arrived), *earlier)


def on_device(green_lesser, coupling, block_list, offsets, shifts, occupation):
    _, energies, _, orbitals, _ = green_lesser.shape
    transfers, listed, _, block, _ = coupling.shape
    assert green_lesser.shape[0] == 1 and energies == SMAX
    momenta, ranks = lax.axis_size("kz"), lax.axis_size("en")
    forward, backward = ring(momenta, 1), ring(momenta, -1)
    scalar_args = (block_list.reshape(-1), offsets, shifts, occupation)
    result = jax.ShapeDtypeStruct(green_lesser.shape, jnp.float32)

    on_chip = both_ways([(i, i + 1) for i in range(0, ranks - 1, 2)])
    between = both_ways([(i, i + 1) for i in range(1, ranks - 1, 2)])
    row = 2 ** math.ceil(math.log2(ranks) / 2)
    turns = [i for i in range(row - 1, ranks - 1, row) if ranks % row == 0]
    across = [(i, j) for i, j in between if min(i, j) not in turns]
    across += [(i, i + row) for i in turns] + [(i + 1, i + 1 - row) for i in turns]
    arriving = [(i + row, i + 1) for i in turns] + [(i + 1 - row, i) for i in turns]

    def call(kernel, out_shape, slots, name, *operands, sums=(), scratch=()):
        return pl.pallas_call(
            kernel,
            in_specs=[SMEM] * 4 + [VMEM] * 2 + [ANY] * len(operands) + [VMEM] * len(sums),
            out_specs=[VMEM] * len(out_shape) if isinstance(out_shape, list) else VMEM,
            out_shape=out_shape,
            scratch_shapes=[*scratch, *term_scratch(slots, coupling.shape, orbitals)],
            compiler_params=LARGE,
            cost_estimate=CHEAP,
            name=name,
        )(*scalar_args, in_vmem(left), in_vmem(right), *operands, *[in_vmem(x) for x in sums])

    def message(place, count, *operands):
        total = pltpu.VMEM((listed, orbitals, 2 * block), jnp.float32)
        kernel = functools.partial(message_kernel, place, 1, row, count)
        return call(
            kernel,
            [pltpu.VMEM((listed, orbitals // count, 2 * block), jnp.bfloat16)] * count,
            transfers,
            "message%d" % place,
            *operands,
            scratch=[total],
        )

    def sums_at(count):
        return pltpu.VMEM((count, *green_lesser.shape[2:]), jnp.float32)

    own1 = take(green_lesser)
    near1 = lax.ppermute(own1, "kz", backward)
    own2 = lax.ppermute(own1, "en", across)
    own0, left, right = prepare(green_lesser, coupling, own1)
    near0 = lax.ppermute(own0, "kz", backward)
    own3 = lax.ppermute(own0, "en", between)
    own_ = lax.ppermute(green_lesser, "en", on_chip)

    mate1 = lax.ppermute(near1, "en", on_chip)
    own_ = after(own_, near1)
    own2 = after(own2, near1)
    relayed2 = lax.ppermute(own2, "en", arriving)
    own = (own_, own0, own1, own2, own3, relayed2)
    (sent0,) = message(0, 1, *own[:-2], relayed2)
    arrived0 = lax.ppermute(sent0, "kz", forward)
    near1 = after(near1, sent0, mate1, cost=CHEAP)
    near2 = lax.ppermute(near1, "en", between)
    sent1, sent2 = message(1, 2, *own)
    arrived1 = lax.ppermute(sent1, "kz", forward)
    arrived2 = lax.ppermute(sent2, "kz", forward)
    near0 = after(near0, sent1, sent0, mate1, cost=CHEAP)
    near3 = lax.ppermute(near0, "en", between)
    mate0 = lax.ppermute(near0, "en", on_chip)
    near2 = after(near2, arrived0, cost=CHEAP)

    near = (mate1, mate0, near0, near1, near2)
    first = functools.partial(first_kernel, 0, -1, row)
    sums = call(first, sums_at(energies), transfers * energies, "first", *own, *near)
    partial = store(0, sums, arrived0, result)
    second = functools.partial(second_kernel, -1, 1)
    sums = call(second, sums_at(1), 1, "second", mate0, near3, sums=[sums])
    partial = store(1, sums, arrived1, result, partial)
    return store(1, sums, arrived2, result, partial, half=1)


def solution(mesh):
    placed = (P("kz", "en", None, None, None), P(), P(), P(), P(), P())
    return jax.shard_map(
        on_device,
        mesh=mesh,
        in_specs=placed,
        out_specs=P("kz", "en", None, None, None),
        check_vma=False,
    )
```
